32 devices in a mesh: row: 8 (over z, y), col: 4 (over x, core).
Axes of the slice: x: 2, y: 2, z: 4, core: 2. Of those that a mesh axis runs over, the one named last changes fastest.
Arguments:
- right_sides: bfloat16 [32, 4, 384, 256], P('row', 'col'), may hold values from -120 to 120
- stiff_diag: bfloat16 [32, 4, 384, 384], P('row', 'col'), may hold values from -0.85 to 7.85
- stiff_upper: bfloat16 [32, 4, 384, 384], P('row', 'col'), may hold values from -0.635 to 0.635
- local_diag: bfloat16 [48, 4, 384, 384], P('row', 'col'), may hold values from -0.089 to 0.79
- local_upper: bfloat16 [40, 4, 384, 384], P('row', 'col'), may hold values from -0.034 to 0.034
- coarse_basis: bfloat16 [8, 4, 6, 1536], P('row', 'col'), may hold values from -0.21875 to 0.21875
- coarse_factor: bfloat16 [192, 192], replicated, may hold values from -0.4375 to 0.4375
Outputs:
- solution: float32 [32, 4, 384, 256], P('row', 'col')
The draws below stay inside these ranges and needn't reach their ends.
All inputs are finite; a program needn't handle non-finite values.
Results may differ from the reference program's by a relative error of at most 0.0018.
Values may be sent and summed in bfloat16 or wider, within the bound.
No kernel may reach another device: no remote copies, remote signals or barrier semaphores. Data moves between devices by JAX's collectives and lax.ppermute only.
A program may use at most 64 MiB of HBM per device.

```python
import jax
import jax.numpy as jnp
from jax import lax

BS = 384
NB = 4
RHS = 256
NCB = 6
ITERS = 2
SUB_ROWS = 8
SUB_COLS = 4
LAYERS = 32
EXT_ROWS = 48
UPPER_ROWS = 40
NCO = 192


def permuted_part(key, count, bound):
    key_perm, key_coef = jax.random.split(key)
    leading = (count, SUB_COLS)
    ordered = jnp.broadcast_to(jnp.arange(BS, dtype=jnp.int32), leading + (BS,))
    shuffled = jax.random.permutation(key_perm, ordered, axis=2, independent=True)
    weights = jax.random.uniform(key_coef, leading + (BS, 1), jnp.float32, -bound, bound)
    col_ids = lax.broadcasted_iota(jnp.int32, leading + (BS, BS), 3)
    return jnp.where(col_ids == shuffled[..., None], weights, 0.0)


def dense_part(key, count, bound):
    return jax.random.uniform(key, (count, SUB_COLS, BS, BS), jnp.float32, -bound, bound)


def symmetric_block(key, count, diag_low, diag_high, perm_bound, dense_bound):
    key_perm = jax.random.fold_in(key, 11)
    key_dense = jax.random.fold_in(key, 12)
    key_diag = jax.random.fold_in(key, 13)
    scattered = permuted_part(key_perm, count, perm_bound)
    noise = dense_part(key_dense, count, dense_bound)
    row_ids = lax.broadcasted_iota(jnp.int32, (count, SUB_COLS, BS, BS), 2)
    col_ids = lax.broadcasted_iota(jnp.int32, (count, SUB_COLS, BS, BS), 3)
    mirrored = jnp.where(row_ids <= col_ids, noise, jnp.swapaxes(noise, 2, 3))
    diag_vals = jax.random.uniform(key_diag, (count, SUB_COLS, BS, 1), jnp.float32, diag_low, diag_high)
    return mirrored + scattered + jnp.swapaxes(scattered, 2, 3) + jnp.where(row_ids == col_ids, diag_vals, 0.0)


def draw_right_sides(key, part):
    key_values = jax.random.fold_in(key, 21)
    key_scale = jax.random.fold_in(key, 22)
    full_shape = (LAYERS, SUB_COLS, BS, RHS)
    layer_pos = lax.broadcasted_iota(jnp.float32, full_shape, 0)
    rising = jnp.exp(jnp.log(3.0) * layer_pos / max(LAYERS - 1, 1))
    spread = jnp.exp(jax.random.uniform(key_scale, (LAYERS, SUB_COLS, BS, 1), jnp.float32, 0.0, jnp.log(10.0)))
    baseline = jnp.clip(jax.random.normal(key_values, full_shape, jnp.float32), -4.0, 4.0)
    return (baseline * spread * rising).astype(jnp.bfloat16)


def draw_stiff_diag(key, part):
    return symmetric_block(jax.random.fold_in(key, 31), LAYERS, 5.5, 7.0, 0.4, 0.05).astype(jnp.bfloat16)


def draw_stiff_upper(key, part):
    scattered = permuted_part(jax.random.fold_in(key, 41), LAYERS, 0.6)
    return (scattered + dense_part(jax.random.fold_in(key, 42), LAYERS, 0.035)).astype(jnp.bfloat16)


def draw_local_diag(key, part):
    return symmetric_block(jax.random.fold_in(key, 51), EXT_ROWS, 0.55, 0.7, 0.04, 0.0087).astype(jnp.bfloat16)


def draw_local_upper(key, part):
    scattered = permuted_part(jax.random.fold_in(key, 61), UPPER_ROWS, 0.03)
    return (scattered + dense_part(jax.random.fold_in(key, 62), UPPER_ROWS, 0.0035)).astype(jnp.bfloat16)


def block_levels(stream_key, extent, shards, low, largest):
    gain, own = 1.0, jax.random.fold_in(stream_key, 6)
    for axis_at, parts in shards:
        draws = jnp.exp(jax.random.uniform(jax.random.fold_in(own, axis_at), (parts,), jnp.float32, low / len(shards), largest / len(shards)))
        gain = gain * jnp.repeat(draws, extent[axis_at] // parts).reshape([-1 if axis == axis_at else 1 for axis in range(len(extent))])
    return gain


def bell_draw(stream_key, dims, scale, reach, shards=(), kind=jnp.bfloat16):
    values = scale * jax.random.normal(stream_key, dims, jnp.float32)
    if shards:
        values = values * block_levels(stream_key, dims, shards, -0.22, 0.18)
    return jnp.clip(values, -reach, reach).astype(kind)


def setup_inputs(seed: int = 0) -> dict:
    keys = jax.random.split(jax.random.key(seed), 8)
    right_sides = draw_right_sides(jax.random.fold_in(keys[7], 71), 0)
    stiff_diag = draw_stiff_diag(jax.random.fold_in(keys[7], 71), 0)
    stiff_upper = draw_stiff_upper(jax.random.fold_in(keys[7], 71), 0)
    local_diag = draw_local_diag(jax.random.fold_in(keys[7], 71), 0)
    local_upper = draw_local_upper(jax.random.fold_in(keys[7], 71), 0)
    coarse_basis = bell_draw(keys[5], (SUB_ROWS, SUB_COLS, NCB, NB * BS), (NB * BS // 2) ** -0.5, 0.21875, ((0, 8), (1, 4)))
    coarse_factor = bell_draw(keys[6], (NCO, NCO), NCO ** -0.5, 0.4375)
    return {"right_sides": right_sides, "stiff_diag": stiff_diag, "stiff_upper": stiff_upper, "local_diag": local_diag, "local_upper": local_upper, "coarse_basis": coarse_basis, "coarse_factor": coarse_factor}


def rounded(values):
    return lax.optimization_barrier(values.astype(jnp.bfloat16))


def multiply(blocks, vectors):
    return jnp.einsum("...ij,...jr->...ir", blocks.astype(jnp.float32), vectors.astype(jnp.float32))


def multiply_transposed(blocks, vectors):
    return jnp.einsum("...ji,...jr->...ir", blocks.astype(jnp.float32), vectors.astype(jnp.float32))


def column_slice(array, column):
    return lax.dynamic_index_in_dim(array, column, 1, keepdims=False)


def per_column(function):
    outputs = lax.map(function, jnp.arange(SUB_COLS, dtype=jnp.int32))
    return jnp.moveaxis(outputs, 0, 1)


def operate(vector, stiff_diag, stiff_upper):
    vec_bf = rounded(vector)

    def one_column(column):
        layers = column_slice(vec_bf, column)
        s_diag = column_slice(stiff_diag, column)
        s_upper = column_slice(stiff_upper, column)
        zero_layer = jnp.zeros((1,) + layers.shape[1:], jnp.float32)
        from_above = jnp.concatenate([multiply(s_upper[:-1], layers[1:]), zero_layer], axis=0)
        from_below = jnp.concatenate([zero_layer, multiply_transposed(s_upper[:-1], layers[:-1])], axis=0)
        return multiply(s_diag, layers) + from_above + from_below

    return per_column(one_column)


def local_solve(res_bf, local_diag, local_upper):
    def one_column(column):
        layers = column_slice(res_bf, column)
        diag_blocks = column_slice(local_diag, column).reshape(SUB_ROWS, NB + 2, BS, BS)
        upper_blocks = column_slice(local_upper, column).reshape(SUB_ROWS, NB + 1, BS, BS)
        padded = jnp.pad(layers, ((1, 1), (0, 0), (0, 0)))
        window_ids = jnp.arange(SUB_ROWS, dtype=jnp.int32)[:, None] * NB + jnp.arange(NB + 2, dtype=jnp.int32)[None, :]
        extended = padded[window_ids]
        zero_layer = jnp.zeros((SUB_ROWS, 1, BS, RHS), jnp.float32)
        solved = multiply(diag_blocks, extended)
        solved = solved + jnp.concatenate([multiply(upper_blocks, extended[:, 1:]), zero_layer], axis=1)
        solved = solved + jnp.concatenate([zero_layer, multiply_transposed(upper_blocks, extended[:, :-1])], axis=1)
        assembled = jnp.zeros(padded.shape, jnp.float32).at[window_ids].add(solved)
        return assembled[1:-1]

    return per_column(one_column)


def coarse_correction(res_bf, coarse_basis, coarse_factor):
    grouped = res_bf.reshape(SUB_ROWS, NB, SUB_COLS, BS, RHS).transpose(0, 2, 1, 3, 4)
    grouped = grouped.reshape(SUB_ROWS, SUB_COLS, NB * BS, RHS)
    coarse_rhs = jnp.einsum("abkn,abnr->abkr", coarse_basis.astype(jnp.float32), grouped.astype(jnp.float32))
    rhs_bf = coarse_rhs.reshape(NCO, RHS).astype(jnp.bfloat16)
    solved = jnp.dot(coarse_factor, rhs_bf, preferred_element_type=jnp.float32)
    coarse_sol = jnp.dot(coarse_factor.T, solved.astype(jnp.bfloat16), preferred_element_type=jnp.float32)
    sol_bf = rounded(coarse_sol).reshape(SUB_ROWS, SUB_COLS, NCB, RHS)
    spread = jnp.einsum("abkn,abkr->abnr", coarse_basis.astype(jnp.float32), sol_bf.astype(jnp.float32))
    spread = spread.reshape(SUB_ROWS, SUB_COLS, NB, BS, RHS).transpose(0, 2, 1, 3, 4)
    return spread.reshape(LAYERS, SUB_COLS, BS, RHS)


def precondition(residual, local_diag, local_upper, coarse_basis, coarse_factor):
    res_bf = rounded(residual)
    local_part = local_solve(res_bf, local_diag, local_upper)
    return local_part + coarse_correction(res_bf, coarse_basis, coarse_factor)


def reference(right_sides, stiff_diag, stiff_upper, local_diag, local_upper, coarse_basis, coarse_factor):
    residual = right_sides.astype(jnp.float32)
    solution = jnp.zeros_like(residual)
    direction = jnp.zeros_like(residual)
    rho_before = jnp.ones((RHS,), jnp.float32)
    for iteration in range(ITERS):
        precond = precondition(residual, local_diag, local_upper, coarse_basis, coarse_factor)
        rho_now = jnp.sum(residual * precond, axis=(0, 1, 2))
        if iteration == 0:
            direction = precond
        else:
            direction = precond + (rho_now / rho_before) * direction
        image_vec = operate(direction, stiff_diag, stiff_upper)
        step_len = rho_now / jnp.sum(direction * image_vec, axis=(0, 1, 2))
        solution = solution + step_len * direction
        residual = residual - step_len * image_vec
        rho_before = rho_now
    return solution
```

```python
import functools

import jax
import jax.numpy as jnp
from jax import lax
from jax.experimental import pallas as pl
from jax.experimental.pallas import tpu as pltpu
from jax.sharding import PartitionSpec as P

BF = jnp.bfloat16
F32 = jnp.float32
ALL = ("row", "col")
PAD = 8


def mm(a, b):
    return lax.dot_general(a, b, (((1,), (0,)), ((), ())), preferred_element_type=F32)


def mmt(a, b):
    return lax.dot_general(a, b, (((0,), (0,)), ((), ())), preferred_element_type=F32)


def is_even():
    return lax.rem(lax.axis_index("row"), 2) == 0


def call(body, outs, args, name, flops=0):
    shapes = [jax.ShapeDtypeStruct(s, d) for s, d in outs]
    total = sum(a.size * a.dtype.itemsize for a in list(args) + shapes)
    return pl.pallas_call(
        body,
        out_shape=shapes,
        in_specs=[pl.BlockSpec(memory_space=pltpu.VMEM)] * len(args),
        out_specs=[pl.BlockSpec(memory_space=pltpu.VMEM)] * len(outs),
        compiler_params=pltpu.CompilerParams(vmem_limit_bytes=24 * 1024 * 1024),
        cost_estimate=pl.CostEstimate(flops=flops, bytes_accessed=total, transcendentals=0),
        name=name,
    )(*args)


def inner_solve(e, ld, lu, y, y0, y5):
    e1, e2, e3, e4 = e[0], e[1], e[2], e[3]
    y0[...] = mm(lu[0], e1)
    y5[...] = mmt(lu[4], e4)
    y[0] = mm(ld[1], e1) + mm(lu[1], e2)
    y[1] = mm(ld[2], e2) + mm(lu[2], e3) + mmt(lu[1], e1)
    y[2] = mm(ld[3], e3) + mm(lu[3], e4) + mmt(lu[2], e2)
    y[3] = mm(ld[4], e4) + mmt(lu[3], e3)


def margin_solve(h2, h1, y0, y5, ld0, ld5, s2, s1):
    even = is_even()
    e0 = jnp.where(even, h2[...], h1[...])
    e5 = jnp.where(even, h1[...], h2[...])
    low = (y0[...] + mm(ld0[0], e0)).astype(BF)
    high = (y5[...] + mm(ld5[0], e5)).astype(BF)
    s2[...] = jnp.where(even, low, high)
    s1[...] = jnp.where(even, high, low)


def add_coarse(h2, h1, y, lu0, lu4, gathered, fpad, fown, basis, p):
    even = is_even()
    e0 = jnp.where(even, h2[...], h1[...])
    e5 = jnp.where(even, h1[...], h2[...])
    g = gathered[...].reshape(-1, gathered.shape[-1])
    v = mm(fpad[...], g).astype(BF)
    u = mmt(fown[...], v).astype(BF)
    size = p.shape[1]
    for k in range(4):
        part = y[k] + mmt(basis[:, k * size : (k + 1) * size], u)
        if k == 0:
            part = part + mmt(lu0[0], e0)
        if k == 3:
            part = part + mm(lu4[0], e5)
        p[k] = part


def join_margins(m2, m1, p, su3, zb, z, s2, s1):
    even = is_even()
    below = jnp.where(even, m2[...], m1[...]).astype(F32)
    above = jnp.where(even, m1[...], m2[...]).astype(F32)
    first = p[0] + below
    last = p[3] + above
    z[0] = first
    z[1] = p[1]
    z[2] = p[2]
    z[3] = last
    fb = first.astype(BF)
    lb = last.astype(BF)
    zb[0] = fb
    zb[1] = p[1].astype(BF)
    zb[2] = p[2].astype(BF)
    zb[3] = lb
    lift = mmt(su3[0], lb).astype(BF)
    s2[...] = jnp.where(even, fb, lift)
    s1[...] = jnp.where(even, lift, fb)


def colsum(x):
    return jnp.sum(x, axis=0, keepdims=True)


def inner_operate(zb, z, r, sd, su, w, wt, rho):
    acc = jnp.zeros_like(rho)
    for k in range(4):
        if k == 0:
            w[k] = mm(su[k], zb[k + 1])
        elif k < 3:
            w[k] = mm(su[k], zb[k + 1]) + mmt(su[k - 1], zb[k - 1])
        else:
            w[k] = mmt(su[k - 1], zb[k - 1])
        own = mm(sd[k], zb[k])
        wt[k] = mmt(sd[k], zb[k]) - own
        w[k] = w[k] + own
        acc = acc + colsum(r[k].astype(F32) * z[k])
    rho[...] = acc


def join_operate(n2, n1, w, su3, basis, wf, wb, g, s2, s1):
    even = is_even()
    below = jnp.where(even, n2[...], n1[...]).astype(F32)
    above = jnp.where(even, n1[...], n2[...])
    first = w[0] + below
    last = w[3] + mm(su3[0], above)
    fb = first.astype(BF)
    lb = last.astype(BF)
    s2[...] = jnp.where(even, fb, lb)
    s1[...] = jnp.where(even, lb, fb)
    wf[0] = first
    wf[1] = w[1]
    wf[2] = w[2]
    wf[3] = last
    wb[0] = fb
    wb[1] = w[1].astype(BF)
    wb[2] = w[2].astype(BF)
    wb[3] = lb
    flat = wb[...].reshape(-1, wb.shape[-1])
    out = mm(basis[...], flat).astype(BF)
    for k in range(g.shape[0]):
        g[k] = out


def coarse_rhs(e, basis, g):
    out = mm(basis[...], e[...].reshape(-1, e.shape[-1])).astype(BF)
    for k in range(g.shape[0]):
        g[k] = out


def join_second(m2, m1, p, q, s):
    even = is_even()
    below = jnp.where(even, m2[...], m1[...]).astype(F32)
    above = jnp.where(even, m1[...], m2[...]).astype(F32)
    first = p[0] + below
    q[0] = first
    q[1] = p[1]
    q[2] = p[2]
    q[3] = p[3] + above
    s[...] = first.astype(BF)


def inner_products(q, z, r, w, wt, sd, su, sums, edge):
    d0 = s1 = s2 = s3 = s5 = jnp.zeros((1, q.shape[-1]), F32)
    for k in range(4):
        qk = q[k]
        qb = qk.astype(BF)
        wk = w[k]
        part = mm(sd[k], qb)
        if k < 3:
            part = part + 2.0 * mm(su[k], q[k + 1].astype(BF))
        else:
            edge[...] = 2.0 * mmt(su[k], qb)
        d0 = d0 + colsum(z[k] * wk)
        s1 = s1 + colsum(r[k].astype(F32) * qk)
        s2 = s2 + colsum(wk * qk)
        s3 = s3 + colsum((wk + wt[k]) * qk)
        s5 = s5 + colsum(qk * part)
    sums[0:1] = d0
    sums[1:2] = s1
    sums[2:3] = s2
    sums[3:4] = s3
    sums[4:5] = s5


def join_sums(t, edge, sums, rho, out):
    s5 = sums[4:5] + colsum(edge[...] * t[...].astype(F32))
    full = jnp.concatenate([rho[...], sums[0:4], s5, rho[...], rho[...]], axis=0)
    for k in range(out.shape[0]):
        out[k] = full


def finish(parts, z, q, x):
    total = parts[0]
    for k in range(1, parts.shape[0]):
        total = total + parts[k]
    rho0, d0, s1, s2, s3, s5 = (total[k : k + 1] for k in range(6))
    a0 = rho0 / d0
    rho1 = a0 * (a0 * s2 - s1)
    grow = 1.0 + rho1 / rho0
    a1 = rho1 / (grow * grow * d0 - grow * a0 * (s3 + s2) + a0 * a0 * s5)
    cz = a0 + a1 * grow
    cq = a1 * a0
    for k in range(4):
        x[k] = cz * z[k] - cq * q[k]


def swap_pairs(count):
    first = [(i, i + 1) for i in range(1, count - 1, 2)]
    second = [(i, i + 1) for i in range(0, count - 1, 2)]
    both = lambda pairs: pairs + [(b, a) for a, b in pairs]
    return both(first), both(second)


def swap(s2, s1):
    odd_even, even_odd = swap_pairs(lax.axis_size("row"))
    return lax.ppermute(s2, "row", odd_even), lax.ppermute(s1, "row", even_odd)


def gather(copies):
    return lax.all_to_all(copies, ALL, 0, 0)


def on_device(rhs, stiff_diag, stiff_upper, local_diag, local_upper, coarse_basis, coarse_factor):
    r = rhs[:, 0]
    sd, su, ld, lu = stiff_diag[:, 0], stiff_upper[:, 0], local_diag[:, 0], local_upper[:, 0]
    layers, size, cols = r.shape
    devices = lax.axis_size("row") * lax.axis_size("col")
    rows = lax.axis_size("row")
    ncb = coarse_basis.shape[2]
    layer = (size, cols)
    own = lax.axis_index("row") * lax.axis_size("col") + lax.axis_index("col")

    even = lax.rem(lax.axis_index("row"), 2) == 0
    low, high = r[0], r[-1]
    h2, h1 = swap(jnp.where(even, low, high), jnp.where(even, high, low))

    basis = jnp.pad(coarse_basis[0, 0], ((0, PAD - ncb), (0, 0)))
    nco = coarse_factor.shape[0]
    wide = lax.broadcasted_iota(jnp.int32, (nco, devices * PAD), 1)
    narrow = lax.broadcasted_iota(jnp.int32, (nco, devices * PAD), 0)
    spread = ((wide // PAD == narrow // ncb) & (wide % PAD == narrow % ncb)).astype(BF)
    fpad = jnp.dot(coarse_factor, spread, preferred_element_type=F32).astype(BF)
    fown = lax.dynamic_slice_in_dim(fpad, own * PAD, PAD, 1)

    ld0, ld5, lu0, lu4, su3 = ld[0:1], ld[-1:], lu[0:1], lu[-1:], su[-1:]
    block = 2 * size * size * cols

    def precondition(e, halo, copies):
        h2, h1 = halo
        gathered = gather(copies)
        y, y0, y5 = call(inner_solve, [((layers,) + layer, F32), (layer, F32), (layer, F32)], (e, ld, lu), "inner_solve", 12 * block)
        sends = call(margin_solve, [(layer, BF)] * 2, (h2, h1, y0, y5, ld0, ld5), "margin_solve", 2 * block)
        margins = swap(*sends)
        (p,) = call(add_coarse, [((layers,) + layer, F32)], (h2, h1, y, lu0, lu4, gathered, fpad, fown, basis), "add_coarse", 3 * block)
        return margins, p

    (copies0,) = call(coarse_rhs, [((devices, PAD, cols), BF)], (r, basis), "coarse_rhs", block // 32)
    (m2, m1), p = precondition(r, (h2, h1), copies0)
    zb, z, s2, s1 = call(
        join_margins, [((layers,) + layer, BF), ((layers,) + layer, F32), (layer, BF), (layer, BF)], (m2, m1, p, su3), "join_margins", block
    )
    n2, n1 = swap(s2, s1)
    w, wt, rho = call(
        inner_operate, [((layers,) + layer, F32)] * 2 + [((1, cols), F32)], (zb, z, r, sd, su), "inner_operate", 14 * block
    )
    wf, wb, copies1, s2, s1 = call(
        join_operate,
        [((layers,) + layer, F32), ((layers,) + layer, BF), ((devices, PAD, cols), BF), (layer, BF), (layer, BF)],
        (n2, n1, w, su3, basis),
        "join_operate",
        block,
    )
    (m2, m1), p = precondition(wb, swap(s2, s1), copies1)
    q, low = call(join_second, [((layers,) + layer, F32), (layer, BF)], (m2, m1, p), "join_second")
    t = lax.ppermute(low, "row", [(i + 1, i) for i in range(rows - 1)])
    sums, edge = call(
        inner_products, [((PAD, cols), F32), (layer, F32)], (q, z, r, wf, wt, sd, su), "inner_products", 8 * block
    )
    (copies,) = call(join_sums, [((devices, PAD, cols), F32)], (t, edge, sums, rho), "join_sums")
    (x,) = call(finish, [((layers,) + layer, F32)], (gather(copies), z, q), "finish")
    return x[:, None]


def solution(mesh):
    split = P("row", "col", None, None)
    return jax.shard_map(on_device, mesh=mesh, in_specs=(split,) * 6 + (P(),), out_specs=split, check_vma=False)
```

```python
import jax
import jax.numpy as jnp
from jax import lax
from jax.experimental import pallas as pl
from jax.experimental.pallas import tpu as pltpu
from jax.sharding import PartitionSpec as P

BF = jnp.bfloat16
F32 = jnp.float32
ALL = ("row", "col")
PAD = 16
LIMIT = 16 * 1024 * 1024
SOLVE_COST = 1200


def mm(a, b):
    return lax.dot_general(a, b, (((1,), (0,)), ((), ())), preferred_element_type=F32)


def mmt(a, b):
    return lax.dot_general(a, b, (((0,), (0,)), ((), ())), preferred_element_type=F32)


def colsum(x):
    return jnp.sum(x, axis=0, keepdims=True)


def is_lower(chain):
    return lax.rem(lax.axis_index("row"), 2) == (0 if chain == 2 else 1)


def pick(from2, from1):
    low2 = is_lower(2)
    return jnp.where(low2, from2, from1), jnp.where(low2, from1, from2)


def call(body, outs, args, name, flops=0, after=None, scratch=(), hbm=()):
    shapes = [jax.ShapeDtypeStruct(d, t) for d, t in outs]
    total = sum(a.size * a.dtype.itemsize for a in list(args) + shapes)
    specs = [pl.BlockSpec(memory_space=pltpu.HBM if i in hbm else pltpu.VMEM) for i in range(len(args))]
    kernel, count = body, len(args)
    if after is not None:
        args = tuple(args) + (after,)
        specs = specs + [pl.BlockSpec(memory_space=pl.ANY)]
        kernel = lambda *refs: body(*refs[:count], *refs[count + 1 :])
    return pl.pallas_call(
        kernel,
        out_shape=shapes,
        in_specs=specs,
        out_specs=[pl.BlockSpec(memory_space=pltpu.VMEM)] * len(outs),
        scratch_shapes=list(scratch),
        compiler_params=pltpu.CompilerParams(vmem_limit_bytes=LIMIT),
        cost_estimate=pl.CostEstimate(flops=flops, bytes_accessed=total, transcendentals=0),
        name=name,
    )(*args)


def load_edges(r, s2, s1, sems):
    last = r.shape[0] - 1
    at = jnp.where(is_lower(2), 0, last)
    copies = [pltpu.make_async_copy(r.at[at], s2, sems.at[0]), pltpu.make_async_copy(r.at[last - at], s1, sems.at[1])]
    for c in copies:
        c.start()
    for c in copies:
        c.wait()


def inner_solve(e, ld, lu, y, ye):
    e1, e2, e3, e4 = e[0], e[1], e[2], e[3]
    ye[0] = mm(lu[0], e1)
    ye[1] = mmt(lu[4], e4)
    y[0] = mm(ld[1], e1) + mm(lu[1], e2)
    y[1] = mm(ld[2], e2) + mm(lu[2], e3) + mmt(lu[1], e1)
    y[2] = mm(ld[3], e3) + mm(lu[3], e4) + mmt(lu[2], e2)
    y[3] = mm(ld[4], e4) + mmt(lu[3], e3)


def margin_solve(chain):
    def body(h, ye, ld, s):
        side = jnp.where(is_lower(chain), 0, 1)
        s[...] = (ye[side] + mm(ld[side * (ld.shape[0] - 1)], h[...])).astype(BF)

    return body


def add_coarse(h2, h1, y, lu, gathered, fpad, fown, basis, p):
    e0, e5 = pick(h2[...], h1[...])
    g = gathered[...].reshape(-1, gathered.shape[-1])
    v = mm(fpad[...], g).astype(BF)
    u = mmt(fown[...], v).astype(BF)
    size = p.shape[1]
    for k in range(4):
        part = y[k] + mmt(basis[:, k * size : (k + 1) * size], u)
        if k == 0:
            part = part + mmt(lu[0], e0)
        if k == 3:
            part = part + mm(lu[4], e5)
        p[k] = part


def join_margin(chain):
    def body(m, p, su, z, s):
        lower = is_lower(chain)

        @pl.when(lower)
        def _():
            edge = p[0] + m[...].astype(F32)
            z[...] = edge
            s[...] = edge.astype(BF)

        @pl.when(jnp.logical_not(lower))
        def _():
            edge = p[3] + m[...].astype(F32)
            z[...] = edge
            s[...] = mmt(su[3], edge.astype(BF)).astype(BF)

    return body


def inner_operate(z2, z1, p, r, sd, su, z, w, wt, rho):
    z[0], z[3] = pick(z2[...], z1[...])
    z[1] = p[1]
    z[2] = p[2]
    acc = jnp.zeros(rho.shape, F32)
    for k in range(4):
        zk = z[k]
        zb = zk.astype(BF)
        if k == 0:
            w[k] = mm(su[k], z[k + 1].astype(BF))
        elif k < 3:
            w[k] = mm(su[k], z[k + 1].astype(BF)) + mmt(su[k - 1], z[k - 1].astype(BF))
        else:
            w[k] = mmt(su[k - 1], z[k - 1].astype(BF))
        own = mm(sd[k], zb)
        wt[k] = mmt(sd[k], zb) - own
        w[k] = w[k] + own
        acc = acc + colsum(r[k].astype(F32) * zk)
    rho[...] = acc


def join_operate(chain):
    def body(n, w, su, edge, s):
        lower = is_lower(chain)

        @pl.when(lower)
        def _():
            out = w[0] + n[...].astype(F32)
            edge[...] = out
            s[...] = out.astype(BF)

        @pl.when(jnp.logical_not(lower))
        def _():
            out = w[3] + mm(su[3], n[...])
            edge[...] = out
            s[...] = out.astype(BF)

    return body


def coarse_rhs(ncb):
    def body(e, basis, g):
        out = mm(basis[...], e[...].reshape(-1, e.shape[-1]))
        out = jnp.concatenate([out, jnp.zeros((PAD - ncb, out.shape[1]), F32)], axis=0).astype(BF)
        for k in range(g.shape[0]):
            g[k] = out

    return body


def prepare(ncb):
    def body(basis, factor, padded, fpad, fown):
        rows = basis[...].astype(F32)
        padded[...] = jnp.concatenate([rows, jnp.zeros((PAD - ncb, rows.shape[1]), F32)], axis=0).astype(BF)
        nco = factor.shape[0]
        own = lax.axis_index("row") * lax.axis_size("col") + lax.axis_index("col")

        def columns(first, width):
            source = lax.broadcasted_iota(jnp.int32, (nco, width), 0)
            target = lax.broadcasted_iota(jnp.int32, (nco, width), 1)
            at = lax.rem(target, PAD)
            match = (source == (first + target // PAD) * ncb + at) & (at < ncb)
            chosen = jnp.where(match, 1.0, 0.0).astype(BF)
            return mm(factor[...], chosen).astype(BF)

        fown[...] = columns(own, PAD)
        width = 128

        def step(i, carry):
            fpad[:, pl.ds(pl.multiple_of(i * width, width), width)] = columns(i * (width // PAD), width)
            return carry

        lax.fori_loop(0, fpad.shape[1] // width, step, 0)

    return body


def three(x):
    parts = []
    for _ in range(3):
        top = x.astype(BF).astype(F32)
        parts.append(top)
        x = x - top
    return parts


def coarse_rhs_sums(w2, w1, w, z, rho, basis, wf, wb, g):
    wf[0], wf[3] = pick(w2[...], w1[...])
    wf[1] = w[1]
    wf[2] = w[2]
    acc = jnp.zeros(rho.shape, F32)
    for k in range(4):
        wk = wf[k]
        wb[k] = wk.astype(BF)
        acc = acc + colsum(wk * z[k])
    out = mm(basis[...], wb[...].reshape(-1, wb.shape[-1]))
    zero = jnp.zeros(rho.shape, F32)
    out = jnp.concatenate([out[:8]] + three(rho[...]) + three(acc) + [zero, zero], axis=0).astype(BF)
    for k in range(g.shape[0]):
        g[k] = out


def join_second(chain):
    def body(m, p, q, s):
        at = jnp.where(is_lower(chain), 0, 3)
        edge = p[at] + m[...].astype(F32)
        q[...] = edge
        s[...] = edge.astype(BF)

    return body


def inner_products(q2, q1, p, z, r, w, wt, sd, su, q, sums, edge):
    q[0], q[3] = pick(q2[...], q1[...])
    q[1] = p[1]
    q[2] = p[2]
    s1 = s2 = s4 = s5 = jnp.zeros((1, q.shape[-1]), F32)
    for k in range(4):
        qk = q[k]
        qb = qk.astype(BF)
        wk = w[k]
        part = mm(sd[k], qb)
        if k < 3:
            part = part + 2.0 * mm(su[k], q[k + 1].astype(BF))
        else:
            edge[...] = 2.0 * mmt(su[k], qb)
        s1 = s1 + colsum(r[k].astype(F32) * qk)
        s2 = s2 + colsum(wk * qk)
        s4 = s4 + colsum((wk + wk + wt[k]) * qk)
        s5 = s5 + colsum(qk * part)
    sums[...] = jnp.concatenate([s1, s2, s4, s5], axis=0)


def join_sums(t2, t1, edge, sums, out):
    _, t = pick(t2[...], t1[...])
    s5 = sums[3:4] + colsum(edge[...] * t.astype(F32))
    full = jnp.concatenate([sums[0:3], s5], axis=0)
    for k in range(out.shape[0]):
        out[k] = full


def finish(parts, early, z, q, x):
    total = parts[0]
    first = early[0].astype(F32)
    for k in range(1, parts.shape[0]):
        total = total + parts[k]
        first = first + early[k].astype(F32)
    rho0 = first[8:9] + first[9:10] + first[10:11]
    d0 = first[11:12] + first[12:13] + first[13:14]
    s1, s2, s4, s5 = (total[k : k + 1] for k in range(4))
    a0 = rho0 / d0
    rho1 = a0 * (a0 * s2 - s1)
    grow = 1.0 + rho1 / rho0
    a1 = rho1 / (grow * grow * d0 - grow * a0 * s4 + a0 * a0 * s5)
    cz = a0 + a1 * grow
    cq = a1 * a0
    for k in range(4):
        x[k] = cz * z[k] - cq * q[k]


def pairs(chain, count):
    return [(i, i + 1) for i in range(1 if chain == 2 else 0, count - 1, 2)]


def swap(chain, x):
    each = pairs(chain, lax.axis_size("row"))
    return lax.ppermute(x, "row", each + [(b, a) for a, b in each])


def send_down(chain, x):
    return lax.ppermute(x, "row", [(b, a) for a, b in pairs(chain, lax.axis_size("row"))])


def gather(copies):
    return lax.all_to_all(copies, ALL, 0, 0)


def on_device(rhs, stiff_diag, stiff_upper, local_diag, local_upper, coarse_basis, coarse_factor):
    layers, _, size, cols = rhs.shape
    devices = lax.axis_size("row") * lax.axis_size("col")
    ncb = coarse_basis.shape[2]
    layer, whole, row = (size, cols), (layers, size, cols), (1, cols)
    block = 2 * size * size * cols
    nco = coarse_factor.shape[0]

    r, sd, su, ld, lu = rhs[:, 0], stiff_diag[:, 0], stiff_upper[:, 0], local_diag[:, 0], local_upper[:, 0]
    s2, s1 = call(load_edges, [(layer, BF), (layer, BF)], (r,), "load_edges", 0, None, [pltpu.SemaphoreType.DMA((2,))], (0,))
    h2, h1 = swap(2, s2), swap(1, s1)
    copies = ((devices, PAD, cols), BF)

    def solve(e, h2, h1, gathered):
        y, ye = call(inner_solve, [(whole, F32), ((2,) + layer, F32)], (e, ld, lu), "inner_solve", SOLVE_COST * block)
        m = []
        for chain, h in ((2, h2), (1, h1)):
            (s,) = call(margin_solve(chain), [(layer, BF)], (h, ye, ld), "margin_solve", block)
            m.append(swap(chain, s))
        (p,) = call(add_coarse, [(whole, F32)], (h2, h1, y, lu, gathered, fpad, fown, basis), "add_coarse", 3 * block)
        return m, p

    raw_basis = coarse_basis[0, 0]
    (g,) = call(coarse_rhs(ncb), [copies], (r, raw_basis), "coarse_rhs", block // 32, s1)
    basis, fpad, fown = call(
        prepare(ncb),
        [((PAD, layers * size), BF), ((nco, devices * PAD), BF), ((nco, PAD), BF)],
        (raw_basis, coarse_factor),
        "prepare",
        block // 8,
        g,
    )
    (m2, m1), p = solve(r, h2, h1, gather(g))
    z2, s2 = call(join_margin(2), [(layer, F32), (layer, BF)], (m2, p, su), "join_margin", block)
    n2 = swap(2, s2)
    z1, s1 = call(join_margin(1), [(layer, F32), (layer, BF)], (m1, p, su), "join_margin", block)
    n1 = swap(1, s1)
    z, wi, wt, rho = call(inner_operate, [(whole, F32)] * 3 + [(row, F32)], (z2, z1, p, r, sd, su), "inner_operate", 14 * block)
    w2, s2 = call(join_operate(2), [(layer, F32), (layer, BF)], (n2, wi, su), "join_operate", block)
    h2 = swap(2, s2)
    w1, s1 = call(join_operate(1), [(layer, F32), (layer, BF)], (n1, wi, su), "join_operate", block)
    h1 = swap(1, s1)
    w, wb, g = call(
        coarse_rhs_sums, [(whole, F32), (whole, BF), copies], (w2, w1, wi, z, rho, basis), "coarse_rhs_sums", block // 32
    )
    early = gather(g)
    (m2, m1), p = solve(wb, h2, h1, early)
    q2, s2 = call(join_second(2), [(layer, F32), (layer, BF)], (m2, p), "join_second")
    t2 = send_down(2, s2)
    q1, s1 = call(join_second(1), [(layer, F32), (layer, BF)], (m1, p), "join_second")
    t1 = send_down(1, s1)
    q, sums, edge = call(
        inner_products, [(whole, F32), ((4, cols), F32), (layer, F32)], (q2, q1, p, z, r, w, wt, sd, su), "inner_products", 8 * block
    )
    (g,) = call(join_sums, [((devices, 4, cols), F32)], (t2, t1, edge, sums), "join_sums")
    x = pl.pallas_call(
        finish,
        out_shape=jax.ShapeDtypeStruct(whole, F32),
        in_specs=[pl.BlockSpec(memory_space=pltpu.VMEM)] * 4,
        out_specs=pl.BlockSpec(memory_space=pltpu.VMEM),
        compiler_params=pltpu.CompilerParams(vmem_limit_bytes=LIMIT),
        name="finish",
    )(gather(g), early, z, q)
    return x[:, None]


def solution(mesh):
    split = P("row", "col", None, None)
    return jax.shard_map(on_device, mesh=mesh, in_specs=(split,) * 6 + (P(),), out_specs=split, check_vma=False)
```

```python
import jax
import jax.numpy as jnp
from jax import lax
from jax.experimental import pallas as pl
from jax.experimental.pallas import tpu as pltpu
from jax.sharding import PartitionSpec as P

BF = jnp.bfloat16
F32 = jnp.float32
ALL = ("row", "col")
PAD = 16
LIMIT = 16 * 1024 * 1024
SCHEDULE_COST = 1200


def mm(a, b):
    return lax.dot_general(a, b, (((1,), (0,)), ((), ())), preferred_element_type=F32)


def mmt(a, b):
    return lax.dot_general(a, b, (((0,), (0,)), ((), ())), preferred_element_type=F32)


def colsum(x):
    return jnp.sum(x, axis=0, keepdims=True)


def is_lower(chain):
    return lax.rem(lax.axis_index("row"), 2) == (0 if chain == 2 else 1)


def goes_on(lower):
    row = lax.axis_index("row")
    return jnp.where(lower, row > 0, row < lax.axis_size("row") - 1)


def kept(x, lower):
    return jnp.where(goes_on(lower), x, jnp.zeros_like(x))


def pick(from2, from1):
    low2 = is_lower(2)
    return jnp.where(low2, from2, from1), jnp.where(low2, from1, from2)


def run_copies(pairs, sems):
    copies = [pltpu.make_async_copy(a, b, sems.at[i]) for i, (a, b) in enumerate(pairs)]
    for c in copies:
        c.start()
    for c in copies:
        c.wait()


def call(body, outs, args, name, flops=0, after=None, scratch=(), hbm=()):
    shapes = [jax.ShapeDtypeStruct(d, t) for d, t in outs]
    total = sum(a.size * a.dtype.itemsize for a in list(args) + shapes)
    count = len(args)
    late = [] if after is None else list(after)
    specs = [pl.BlockSpec(memory_space=pltpu.HBM if i in hbm else pltpu.VMEM) for i in range(count)]

    def kernel(*refs):
        body(*refs[:count], *refs[count + len(late) :])

    return pl.pallas_call(
        kernel,
        out_shape=shapes,
        in_specs=specs + [pl.BlockSpec(memory_space=pl.ANY)] * len(late),
        out_specs=[pl.BlockSpec(memory_space=pltpu.VMEM)] * len(outs),
        scratch_shapes=list(scratch),
        compiler_params=pltpu.CompilerParams(vmem_limit_bytes=LIMIT),
        cost_estimate=pl.CostEstimate(flops=flops, bytes_accessed=total, transcendentals=0),
        name=name,
    )(*args, *late)


def mark(out):
    out[...] = jnp.zeros(out.shape, F32)


def load_edge(chain):
    def body(r, s, sems):
        run_copies([(r.at[jnp.where(is_lower(chain), 0, r.shape[0] - 1)], s)], sems)

    return body


def margin_solve(chain):
    def body(h, e, ld, lu, s, diag, upper, sems):
        lower = is_lower(chain)
        at = [jnp.where(lower, 0, m.shape[0] - 1) for m in (ld, lu)]
        run_copies([(ld.at[at[0]], diag), (lu.at[at[1]], upper)], sems)

        @pl.when(lower)
        def _():
            s[...] = (mm(diag[...], h[...]) + mm(upper[...], e[...])).astype(BF)

        @pl.when(jnp.logical_not(lower))
        def _():
            s[...] = (mm(diag[...], h[...]) + mmt(upper[...], e[...])).astype(BF)

    return body


def solve_layers(h2, h1, o2, o1, e, ld, lu, gathered, fpad, fown, basis, p):
    e0, e5 = pick(h2[...], h1[...])
    e0, e5 = kept(e0, True), kept(e5, False)
    e1, e4 = pick(o2[...], o1[...])
    e2, e3 = e[1], e[2]
    g = gathered[...].reshape(-1, gathered.shape[-1])
    v = mm(fpad[...], g).astype(BF)
    u = mmt(fown[...], v).astype(BF)
    size = p.shape[1]
    p[0] = mm(ld[1], e1) + mm(lu[1], e2) + mmt(lu[0], e0)
    p[1] = mm(ld[2], e2) + mm(lu[2], e3) + mmt(lu[1], e1)
    p[2] = mm(ld[3], e3) + mm(lu[3], e4) + mmt(lu[2], e2)
    p[3] = mm(ld[4], e4) + mm(lu[4], e5) + mmt(lu[3], e3)
    for k in range(4):
        p[k] = p[k] + mmt(basis[:, k * size : (k + 1) * size], u)


def join_margin(chain):
    def body(m, p, su, z, s):
        lower = is_lower(chain)
        edge = p[jnp.where(lower, 0, 3)] + kept(m[...], lower).astype(F32)
        z[...] = edge
        s[...] = edge.astype(BF)

        @pl.when(jnp.logical_not(lower))
        def _():
            s[...] = mmt(su[3], edge.astype(BF)).astype(BF)

    return body


def inner_operate(z2, z1, p, r, sd, su, z, w, wb, rho):
    z[0], z[3] = pick(z2[...], z1[...])
    z[1] = p[1]
    z[2] = p[2]
    acc = jnp.zeros(rho.shape, F32)
    for k in range(4):
        zk = z[k]
        acc = acc + colsum(r[k].astype(F32) * zk)
        w[k] = mm(sd[k], zk.astype(BF))
        if k < 3:
            w[k] = w[k] + mm(su[k], z[k + 1].astype(BF))
        if k > 0:
            w[k] = w[k] + mmt(su[k - 1], z[k - 1].astype(BF))
        wb[k] = w[k].astype(BF)
    rho[...] = acc


def join_operate(chain):
    def body(n, w, su, edge, s):
        lower = is_lower(chain)
        term = kept(n[...], lower)

        @pl.when(lower)
        def _():
            edge[...] = w[0] + term.astype(F32)

        @pl.when(jnp.logical_not(lower))
        def _():
            edge[...] = w[3] + mm(su[3], term)

        s[...] = edge[...].astype(BF)

    return body


def coarse_rhs(ncb):
    def body(e, basis, g, held, sems):
        run_copies([(e, held)], sems)
        out = mm(basis[...], held[...].reshape(-1, e.shape[-1]))
        out = jnp.concatenate([out, jnp.zeros((PAD - ncb, out.shape[1]), F32)], axis=0).astype(BF)
        for k in range(g.shape[0]):
            g[k] = out

    return body


def prepare(ncb):
    def body(basis, factor, padded, fpad, fown):
        rows = basis[...].astype(F32)
        padded[...] = jnp.concatenate([rows, jnp.zeros((PAD - ncb, rows.shape[1]), F32)], axis=0).astype(BF)
        nco = factor.shape[0]
        own = lax.axis_index("row") * lax.axis_size("col") + lax.axis_index("col")

        def columns(first, width):
            source = lax.broadcasted_iota(jnp.int32, (nco, width), 0)
            target = lax.broadcasted_iota(jnp.int32, (nco, width), 1)
            at = lax.rem(target, PAD)
            match = (source == (first + target // PAD) * ncb + at) & (at < ncb)
            chosen = jnp.where(match, 1.0, 0.0).astype(BF)
            return mm(factor[...], chosen).astype(BF)

        fown[...] = columns(own, PAD)
        width = 128

        def step(i, carry):
            fpad[:, pl.ds(pl.multiple_of(i * width, width), width)] = columns(i * (width // PAD), width)
            return carry

        lax.fori_loop(0, fpad.shape[1] // width, step, 0)

    return body


def three(x):
    parts = []
    for _ in range(3):
        top = x.astype(BF).astype(F32)
        parts.append(top)
        x = x - top
    return parts


def coarse_rhs_sums(ncb):
    def body(w2, w1, w, z2, z1, p, rho, basis, g):
        ends = [pick(w2[...], w1[...]), pick(z2[...], z1[...])]
        acc = jnp.zeros(rho.shape, F32)
        out = jnp.zeros((ncb, rho.shape[1]), F32)
        size = w.shape[1]
        for k in range(4):
            wk, zk = (w[k], p[k]) if 0 < k < 3 else (pair[k // 3] for pair in ends)
            out = out + mm(basis[:, k * size : (k + 1) * size], wk.astype(BF))
            acc = acc + colsum(wk * zk)
        rows = [out, jnp.zeros((8 - ncb, out.shape[1]), F32)] + three(rho[...]) + three(acc)
        out = jnp.concatenate(rows + [jnp.zeros((2, out.shape[1]), F32)], axis=0).astype(BF)
        for k in range(g.shape[0]):
            g[k] = out

    return body


def join_second(chain):
    def body(m, p, su, q, s, product):
        lower = is_lower(chain)
        half = s.shape[1]
        edge = p[jnp.where(lower, 0, 3)] + kept(m[...], lower).astype(F32)
        q[...] = edge
        product[...] = edge

        @pl.when(lower)
        def _():
            s[...] = edge[:, :half].astype(BF)

        @pl.when(jnp.logical_not(lower))
        def _():
            out = 2.0 * mmt(su[3], edge.astype(BF))
            product[...] = out
            s[...] = out[:, half:].astype(BF)

    return body


def inner_products(q2, q1, o2, o1, p, z, r, w, sd, su, q, sums):
    q[0], q[3] = pick(q2[...], q1[...])
    q[1] = p[1]
    q[2] = p[2]
    ends = pick(o2[...], o1[...])
    s1 = s2 = s4 = s5 = jnp.zeros((1, q.shape[-1]), F32)
    for k in range(4):
        qk = q[k]
        qb = qk.astype(BF)
        wk = (w[k] if 0 < k < 3 else ends[k // 3]).astype(F32)
        zk = z[k]
        own = mm(sd[k], qb)
        s5 = s5 + colsum(qk * own)
        s4 = s4 + colsum(zk * own)
        s4 = s4 + colsum((wk + wk - mm(sd[k], zk.astype(BF))) * qk)
        if k < 3:
            s5 = s5 + 2.0 * colsum(qk * mm(su[k], q[k + 1].astype(BF)))
        s1 = s1 + colsum(r[k].astype(F32) * qk)
        s2 = s2 + colsum(wk * qk)
    sums[...] = jnp.concatenate([s1, s2, s4, s5], axis=0)


def join_sums(t2, t1, c2, c1, sums, out):
    low_in, high_in = pick(t2[...], t1[...])
    low, high = pick(c2[...], c1[...])
    half = low_in.shape[1]
    above = colsum(high[:, :half] * kept(high_in, False).astype(F32))
    below = colsum(low[:, half:] * kept(low_in, True).astype(F32))
    s5 = sums[3:4] + jnp.concatenate([above, below], axis=1)
    full = jnp.concatenate([sums[0:3], s5], axis=0)
    for k in range(out.shape[0]):
        out[k] = full


def finish(parts, early, z, q, x):
    total = parts[0]
    first = early[0].astype(F32)
    for k in range(1, parts.shape[0]):
        total = total + parts[k]
        first = first + early[k].astype(F32)
    rho0 = first[8:9] + first[9:10] + first[10:11]
    d0 = first[11:12] + first[12:13] + first[13:14]
    s1, s2, s4, s5 = (total[k : k + 1] for k in range(4))
    a0 = rho0 / d0
    rho1 = a0 * (a0 * s2 - s1)
    grow = 1.0 + rho1 / rho0
    a1 = rho1 / (grow * grow * d0 - grow * a0 * s4 + a0 * a0 * s5)
    cz = a0 + a1 * grow
    cq = a1 * a0
    for k in range(4):
        x[k] = cz * z[k] - cq * q[k]


def swap(chain, x):
    rows, cols = lax.axis_size("row"), lax.axis_size("col")
    moves = []
    for row in range(rows):
        other = row + 1 if (row % 2 == 0) == (chain == 1) else row - 1
        for col in range(cols):
            inside = 0 <= other < rows
            to = (other, col) if inside else (row, min(col ^ 1, cols - 1))
            moves.append((row * cols + col, to[0] * cols + to[1]))
    return lax.ppermute(x, ALL, moves)


def gather(copies):
    return lax.all_to_all(copies, ALL, 0, 0)


def on_device(rhs, stiff_diag, stiff_upper, local_diag, local_upper, coarse_basis, coarse_factor):
    layers, _, size, cols = rhs.shape
    devices = lax.axis_size("row") * lax.axis_size("col")
    ncb, nco = coarse_basis.shape[2], coarse_factor.shape[0]
    layer, whole, row = (size, cols), (layers, size, cols), (1, cols)
    copies = ((devices, PAD, cols), BF)
    edge = [(layer, F32), (layer, BF)]
    block = 2 * size * size * cols
    dma = lambda n: pltpu.SemaphoreType.DMA((n,))
    r, sd, su, ld, lu = rhs[:, 0], stiff_diag[:, 0], stiff_upper[:, 0], local_diag[:, 0], local_upper[:, 0]
    raw_basis = coarse_basis[0, 0]

    def margins(h2, h1, o2, o1, order):
        blocks = [pltpu.VMEM((size, size), BF)] * 2 + [dma(2)]
        take = lambda chain, h, o, after: call(
            margin_solve(chain), [(layer, BF)], (h, o, ld, lu), "margin_solve", 2 * block, after, blocks, (2, 3)
        )[0]
        s2 = take(2, h2, o2, order)
        s1 = take(1, h1, o1, [s2])
        return swap(2, s2), swap(1, s1)

    def beside(g):
        return call(mark, [((8, 128), F32)], (), "beside", SCHEDULE_COST * block, [g])[0]

    def solve(h2, h1, o2, o1, e, gathered):
        args = (h2, h1, o2, o1, e, ld, lu, gathered, fpad, fown, basis)
        return call(solve_layers, [(whole, F32)], args, "solve_layers", 12 * block)[0]

    (s2,) = call(load_edge(2), [(layer, BF)], (r,), "load_edge", 0, None, [dma(1)], (0,))
    h2 = swap(2, s2)
    (s1,) = call(load_edge(1), [(layer, BF)], (r,), "load_edge", 0, [s2], [dma(1)], (0,))
    h1 = swap(1, s1)
    (g,) = call(coarse_rhs(ncb), [copies], (r, raw_basis), "coarse_rhs", block // 32, [s1], [pltpu.VMEM(whole, BF), dma(1)], (0,))
    gathered = gather(g)
    m2, m1 = margins(h2, h1, s2, s1, [beside(g)])
    basis, fpad, fown = call(
        prepare(ncb),
        [((PAD, layers * size), BF), ((nco, devices * PAD), BF), ((nco, PAD), BF)],
        (raw_basis, coarse_factor),
        "prepare",
        block // 8,
        [gathered],
    )
    p = solve(h2, h1, s2, s1, r, gathered)
    z2, s2 = call(join_margin(2), edge, (m2, p, su), "join_margin", block)
    z1, s1 = call(join_margin(1), edge, (m1, p, su), "join_margin", block, [s2])
    n2, n1 = swap(2, s2), swap(1, s1)
    z, wi, w, rho = call(
        inner_operate, [(whole, F32)] * 2 + [(whole, BF), (row, F32)], (z2, z1, p, r, sd, su), "inner_operate", 10 * block
    )
    w2, o2 = call(join_operate(2), edge, (n2, wi, su), "join_operate", block)
    w1, o1 = call(join_operate(1), edge, (n1, wi, su), "join_operate", block, [o2])
    h2, h1 = swap(2, o2), swap(1, o1)
    (g,) = call(coarse_rhs_sums(ncb), [copies], (w2, w1, wi, z2, z1, p, rho, raw_basis), "coarse_rhs_sums", block // 32)
    early = gather(g)
    m2, m1 = margins(h2, h1, o2, o1, [beside(g)])
    p = solve(h2, h1, o2, o1, w, early)
    half = [(layer, F32), ((size, cols // 2), BF), (layer, F32)]
    q2, s2, c2 = call(join_second(2), half, (m2, p, su), "join_second", block)
    q1, s1, c1 = call(join_second(1), half, (m1, p, su), "join_second", block, [s2])
    t2, t1 = swap(2, s2), swap(1, s1)
    q, sums = call(
        inner_products,
        [(whole, F32), ((4, cols), F32)],
        (q2, q1, o2, o1, p, z, r, w, sd, su),
        "inner_products",
        12 * block,
    )
    (g,) = call(join_sums, [((devices, 4, cols), F32)], (t2, t1, c2, c1, sums), "join_sums")
    (x,) = call(finish, [(whole, F32)], (gather(g), early, z, q), "finish")
    return x[:, None]


def solution(mesh):
    split = P("row", "col", None, None)
    return jax.shard_map(on_device, mesh=mesh, in_specs=(split,) * 6 + (P(),), out_specs=split, check_vma=False)
```

```python
import math

import jax
import jax.numpy as jnp
from jax import lax
from jax.experimental import pallas as pl
from jax.experimental.pallas import tpu as pltpu
from jax.sharding import PartitionSpec as P

BF = jnp.bfloat16
F32 = jnp.float32
ALL = ("row", "col")
PAD = 16
LIMIT = 16 * 1024 * 1024
SCHEDULE_COST = 1200


def mm(a, b):
    return lax.dot_general(a, b, (((1,), (0,)), ((), ())), preferred_element_type=F32)


def mmt(a, b):
    return lax.dot_general(a, b, (((0,), (0,)), ((), ())), preferred_element_type=F32)


def colsum(x):
    return jnp.sum(x, axis=0, keepdims=True)


def is_lower(chain):
    return lax.rem(lax.axis_index("row"), 2) == (0 if chain == 2 else 1)


def goes_on(lower):
    row = lax.axis_index("row")
    return jnp.where(lower, row > 0, row < lax.axis_size("row") - 1)


def kept(x, lower):
    return jnp.where(goes_on(lower), x, jnp.zeros_like(x))


def pick(from2, from1):
    low2 = is_lower(2)
    return jnp.where(low2, from2, from1), jnp.where(low2, from1, from2)


def nbytes(shape, dtype):
    return math.prod(shape) * jnp.dtype(dtype).itemsize


def run_copies(pairs, sems):
    copies = [pltpu.make_async_copy(a, b, sems.at[i]) for i, (a, b) in enumerate(pairs)]
    for c in copies:
        c.start()
    for c in copies:
        c.wait()


def call(body, outs, args, name, flops=0, after=(), scratch=(), hbm=(), far=()):
    shapes = [pltpu.HBM(d, t) if i in far else jax.ShapeDtypeStruct(d, t) for i, (d, t) in enumerate(outs)]
    total = sum(nbytes(a.shape, a.dtype) for a in args)
    room = sum(nbytes(a.shape, a.dtype) for i, a in enumerate(args) if i not in hbm)
    room += sum(nbytes(d, t) for i, (d, t) in enumerate(outs) if i not in far)
    room += sum(nbytes(a.shape, a.dtype) for a in scratch if jnp.issubdtype(a.dtype, jnp.floating))
    args = [pltpu.with_memory_space_constraint(a, pltpu.HBM) if i in hbm else a for i, a in enumerate(args)]
    count, late = len(args), len(after)

    def kernel(*refs):
        body(*refs[:count], *refs[count + late :])

    space = lambda i, there: pl.BlockSpec(memory_space=pltpu.HBM if i in there else pltpu.VMEM)
    return pl.pallas_call(
        kernel,
        out_shape=shapes,
        in_specs=[space(i, hbm) for i in range(count)] + [pl.BlockSpec(memory_space=pl.ANY)] * late,
        out_specs=[space(i, far) for i in range(len(outs))],
        scratch_shapes=list(scratch),
        compiler_params=pltpu.CompilerParams(vmem_limit_bytes=max(LIMIT, room + LIMIT // 2)),
        cost_estimate=pl.CostEstimate(flops=flops, bytes_accessed=total, transcendentals=0),
        name=name,
    )(*args, *after)


def load_edge(chain):
    def body(r, s, sems):
        run_copies([(r.at[jnp.where(is_lower(chain), 0, r.shape[0] - 1)], s)], sems)

    return body


def load_outer(ld, lu, d2, u2, d1, u1, sems):
    lower = is_lower(2)
    at = [jnp.where(lower, 0, m.shape[0] - 1) for m in (ld, lu)]
    to = [m.shape[0] - 1 - i for m, i in zip((ld, lu), at)]
    blocks = [(ld.at[at[0]], d2), (lu.at[at[1]], u2), (ld.at[to[0]], d1), (lu.at[to[1]], u1)]
    run_copies(blocks, sems)


def margin_solve(chain, fetch):
    def body(h, e, diag, upper, s, *held):
        lower = is_lower(chain)
        if fetch:
            run_copies([(h, held[0]), (e, held[1])], held[2])
            h, e = held[:2]

        @pl.when(lower)
        def _():
            s[...] = (mm(diag[...], h[...]) + mm(upper[...], e[...])).astype(BF)

        @pl.when(jnp.logical_not(lower))
        def _():
            s[...] = (mm(diag[...], h[...]) + mmt(upper[...], e[...])).astype(BF)

    return body


def solve_layers(*refs):
    count = 11
    far, p, near, sems = refs[:count], refs[count], refs[count + 1 : 2 * count + 1], refs[-1]
    copies = [pltpu.make_async_copy(a, b, sems.at[i]) for i, (a, b) in enumerate(zip(far, near))]
    for c in copies:
        c.start()
    gathered, fpad, fown, basis, h2, h1, o2, o1, e, ld, lu = near
    for c in copies[:4]:
        c.wait()
    g = gathered[...].reshape(-1, gathered.shape[-1])
    v = mm(fpad[...], g).astype(BF)
    u = mmt(fown[...], v).astype(BF)
    size = p.shape[1]
    for c in copies[4:10]:
        c.wait()
    e0, e5 = pick(h2[...], h1[...])
    e0, e5 = kept(e0, True), kept(e5, False)
    e1, e4 = pick(o2[...], o1[...])
    e2, e3 = e[1], e[2]
    for k, x in enumerate((e1, e2, e3, e4)):
        p[k] = mm(ld[k + 1], x) + mmt(basis[:, k * size : (k + 1) * size], u)
    copies[10].wait()
    p[0] = p[0] + mm(lu[1], e2) + mmt(lu[0], e0)
    p[1] = p[1] + mm(lu[2], e3) + mmt(lu[1], e1)
    p[2] = p[2] + mm(lu[3], e4) + mmt(lu[2], e2)
    p[3] = p[3] + mm(lu[4], e5) + mmt(lu[3], e3)


def join_margin(chain):
    def body(m, p, su, z, s):
        lower = is_lower(chain)
        edge = p[jnp.where(lower, 0, 3)] + kept(m[...], lower).astype(F32)
        z[...] = edge
        s[...] = edge.astype(BF)

        @pl.when(jnp.logical_not(lower))
        def _():
            s[...] = mmt(su[3], edge.astype(BF)).astype(BF)

    return body


def inner_operate(z2, z1, p, r, sd, su, z, w, wb, rho):
    z[0], z[3] = pick(z2[...], z1[...])
    z[1] = p[1]
    z[2] = p[2]
    acc = jnp.zeros(rho.shape, F32)
    for k in range(4):
        zk = z[k]
        acc = acc + colsum(r[k].astype(F32) * zk)
        w[k] = mm(sd[k], zk.astype(BF))
        if k < 3:
            w[k] = w[k] + mm(su[k], z[k + 1].astype(BF))
        if k > 0:
            w[k] = w[k] + mmt(su[k - 1], z[k - 1].astype(BF))
        wb[k] = w[k].astype(BF)
    rho[...] = acc


def join_operate(chain):
    def body(n, w, su, edge, s):
        lower = is_lower(chain)
        term = kept(n[...], lower)

        @pl.when(lower)
        def _():
            edge[...] = w[0] + term.astype(F32)

        @pl.when(jnp.logical_not(lower))
        def _():
            edge[...] = w[3] + mm(su[3], term)

        s[...] = edge[...].astype(BF)

    return body


def coarse_rhs(ncb):
    def body(e, basis, g, held, rows, block, sems):
        run_copies([(e, held), (basis, rows)], sems)
        out = mm(rows[...], held[...].reshape(-1, e.shape[-1]))
        out = jnp.concatenate([out, jnp.zeros((PAD - ncb, out.shape[1]), F32)], axis=0).astype(BF)
        for k in range(g.shape[0]):
            block[k] = out
        run_copies([(block, g)], sems)

    return body


def prepare(ncb):
    def body(basis, factor, padded_far, fpad_far, fown_far, padded, fpad, fown, sems):
        rows = basis[...].astype(F32)
        padded[...] = jnp.concatenate([rows, jnp.zeros((PAD - ncb, rows.shape[1]), F32)], axis=0).astype(BF)
        nco = factor.shape[0]
        own = lax.axis_index("row") * lax.axis_size("col") + lax.axis_index("col")

        def columns(first, width):
            source = lax.broadcasted_iota(jnp.int32, (nco, width), 0)
            target = lax.broadcasted_iota(jnp.int32, (nco, width), 1)
            at = lax.rem(target, PAD)
            match = (source == (first + target // PAD) * ncb + at) & (at < ncb)
            chosen = jnp.where(match, 1.0, 0.0).astype(BF)
            return mm(factor[...], chosen).astype(BF)

        fown[...] = columns(own, PAD)
        width = 128

        def step(i, carry):
            fpad[:, pl.ds(pl.multiple_of(i * width, width), width)] = columns(i * (width // PAD), width)
            return carry

        lax.fori_loop(0, fpad.shape[1] // width, step, 0)
        run_copies([(padded, padded_far), (fpad, fpad_far), (fown, fown_far)], sems)

    return body


def three(x):
    parts = []
    for _ in range(3):
        top = x.astype(BF).astype(F32)
        parts.append(top)
        x = x - top
    return parts


def coarse_rhs_sums(ncb):
    def body(w2, w1, w, z2, z1, p, rho, basis, g, block, sems):
        ends = [pick(w2[...], w1[...]), pick(z2[...], z1[...])]
        acc = jnp.zeros(rho.shape, F32)
        out = jnp.zeros((ncb, rho.shape[1]), F32)
        size = w.shape[1]
        for k in range(4):
            wk, zk = (w[k], p[k]) if 0 < k < 3 else (pair[k // 3] for pair in ends)
            out = out + mm(basis[:, k * size : (k + 1) * size], wk.astype(BF))
            acc = acc + colsum(wk * zk)
        rows = [out, jnp.zeros((8 - ncb, out.shape[1]), F32)] + three(rho[...]) + three(acc)
        out = jnp.concatenate(rows + [jnp.zeros((2, out.shape[1]), F32)], axis=0).astype(BF)
        for k in range(g.shape[0]):
            block[k] = out
        run_copies([(block, g)], sems)

    return body


def join_second(chain):
    def body(m, p, su, q, s, product):
        lower = is_lower(chain)
        half = s.shape[1]
        edge = p[jnp.where(lower, 0, 3)] + kept(m[...], lower).astype(F32)
        q[...] = edge
        product[...] = edge

        @pl.when(lower)
        def _():
            s[...] = edge[:, :half].astype(BF)

        @pl.when(jnp.logical_not(lower))
        def _():
            out = 2.0 * mmt(su[3], edge.astype(BF))
            product[...] = out
            s[...] = out[:, half:].astype(BF)

    return body


def inner_products(q2, q1, o2, o1, p, z, r, w, sd, su, early, q, kept_z, first, sums):
    q[0], q[3] = pick(q2[...], q1[...])
    q[1] = p[1]
    q[2] = p[2]
    ends = pick(o2[...], o1[...])
    kept_z[...] = z[...]
    total = early[0].astype(F32)
    for k in range(1, early.shape[0]):
        total = total + early[k].astype(F32)
    first[...] = total
    s1 = s2 = s4 = s5 = jnp.zeros((1, q.shape[-1]), F32)
    for k in range(4):
        qk = q[k]
        qb = qk.astype(BF)
        wk = (w[k] if 0 < k < 3 else ends[k // 3]).astype(F32)
        zk = z[k]
        own = mm(sd[k], qb)
        s5 = s5 + colsum(qk * own)
        s4 = s4 + colsum(zk * own)
        s4 = s4 + colsum((wk + wk - mm(sd[k], zk.astype(BF))) * qk)
        if k < 3:
            s5 = s5 + 2.0 * colsum(qk * mm(su[k], q[k + 1].astype(BF)))
        s1 = s1 + colsum(r[k].astype(F32) * qk)
        s2 = s2 + colsum(wk * qk)
    sums[...] = jnp.concatenate([s1, s2, s4, s5], axis=0)


def join_sums(t2, t1, c2, c1, sums, out):
    low_in, high_in = pick(t2[...], t1[...])
    low, high = pick(c2[...], c1[...])
    half = low_in.shape[1]
    above = colsum(high[:, :half] * kept(high_in, False).astype(F32))
    below = colsum(low[:, half:] * kept(low_in, True).astype(F32))
    s5 = sums[3:4] + jnp.concatenate([above, below], axis=1)
    full = jnp.concatenate([sums[0:3], s5], axis=0)
    for k in range(out.shape[0]):
        out[k] = full


def finish(parts, first, z, q, x):
    total = parts[0]
    for k in range(1, parts.shape[0]):
        total = total + parts[k]
    rho0 = first[8:9] + first[9:10] + first[10:11]
    d0 = first[11:12] + first[12:13] + first[13:14]
    s1, s2, s4, s5 = (total[k : k + 1] for k in range(4))
    a0 = rho0 / d0
    rho1 = a0 * (a0 * s2 - s1)
    grow = 1.0 + rho1 / rho0
    a1 = rho1 / (grow * grow * d0 - grow * a0 * s4 + a0 * a0 * s5)
    cz = a0 + a1 * grow
    cq = a1 * a0
    for k in range(4):
        x[k] = cz * z[k] - cq * q[k]


def swap(chain, x):
    rows, cols = lax.axis_size("row"), lax.axis_size("col")
    moves = []
    for row in range(rows):
        other = row + 1 if (row % 2 == 0) == (chain == 1) else row - 1
        for col in range(cols):
            inside = 0 <= other < rows
            to = (other, col) if inside else (row, min(col ^ 1, cols - 1))
            moves.append((row * cols + col, to[0] * cols + to[1]))
    return lax.ppermute(x, ALL, moves)


def gather(copies):
    return lax.all_to_all(copies, ALL, 0, 0)


def on_device(rhs, stiff_diag, stiff_upper, local_diag, local_upper, coarse_basis, coarse_factor):
    layers, _, size, cols = rhs.shape
    devices = lax.axis_size("row") * lax.axis_size("col")
    ncb, nco = coarse_basis.shape[2], coarse_factor.shape[0]
    layer, whole, row = (size, cols), (layers, size, cols), (1, cols)
    copies = ((devices, PAD, cols), BF)
    edge = [(layer, F32), (layer, BF)]
    block = 2 * size * size * cols
    dma = lambda n: pltpu.SemaphoreType.DMA((n,))
    r, sd, su, ld, lu = rhs[:, 0], stiff_diag[:, 0], stiff_upper[:, 0], local_diag[:, 0], local_upper[:, 0]
    raw_basis = coarse_basis[0, 0]

    def margins(h2, h1, o2, o1, g, fetch):
        g = pltpu.with_memory_space_constraint(g, pltpu.HBM)
        d2, u2, d1, u1 = call(
            load_outer, [((size, size), BF)] * 4, (ld, lu), "load_outer", SCHEDULE_COST * block, [g], [dma(4)], (0, 1)
        )
        held, far = ([pltpu.VMEM(layer, BF)] * 2 + [dma(2)], (0, 1)) if fetch else ((), ())
        take = lambda chain, args, after: call(
            margin_solve(chain, fetch), [(layer, BF)], args, "margin_solve", 2 * block, after, held, far
        )[0]
        s2 = take(2, (h2, o2, d2, u2), ())
        s1 = take(1, (h1, o1, d1, u1), [s2])
        return swap(2, s2), swap(1, s1), s1

    def solve(h2, h1, o2, o1, e, gathered):
        args = (gathered, fpad, fown, basis, h2, h1, o2, o1, e, ld, lu)
        held = [pltpu.VMEM(a.shape, a.dtype) for a in args] + [dma(len(args))]
        return call(solve_layers, [(whole, F32)], args, "solve_layers", 12 * block, (), held, range(len(args)))[0]

    (s2,) = call(load_edge(2), [(layer, BF)], (r,), "load_edge", 0, (), [dma(1)], (0,))
    h2 = swap(2, s2)
    (s1,) = call(load_edge(1), [(layer, BF)], (r,), "load_edge", 0, [s2], [dma(1)], (0,))
    h1 = swap(1, s1)
    held = [pltpu.VMEM(whole, BF), pltpu.VMEM(raw_basis.shape, BF), pltpu.VMEM(*copies), dma(2)]
    (g,) = call(coarse_rhs(ncb), [copies], (r, raw_basis), "coarse_rhs", block // 32, [s1], held, (0, 1), (0,))
    gathered = gather(g)
    m2, m1, last = margins(h2, h1, s2, s1, g, False)
    shapes = [((PAD, layers * size), BF), ((nco, devices * PAD), BF), ((nco, PAD), BF)]
    held = [pltpu.VMEM(*shape) for shape in shapes] + [dma(3)]
    basis, fpad, fown = call(
        prepare(ncb), shapes, (raw_basis, coarse_factor), "prepare", block // 8, [last], held, (), (0, 1, 2)
    )
    p = solve(h2, h1, s2, s1, r, gathered)
    z2, s2 = call(join_margin(2), edge, (m2, p, su), "join_margin", block)
    z1, s1 = call(join_margin(1), edge, (m1, p, su), "join_margin", block, [s2])
    n2, n1 = swap(2, s2), swap(1, s1)
    z, wi, w, rho = call(
        inner_operate, [(whole, F32)] * 2 + [(whole, BF), (row, F32)], (z2, z1, p, r, sd, su), "inner_operate", 10 * block
    )
    w2, o2 = call(join_operate(2), edge, (n2, wi, su), "join_operate", block)
    w1, o1 = call(join_operate(1), edge, (n1, wi, su), "join_operate", block, [o2])
    h2, h1 = swap(2, o2), swap(1, o1)
    (g,) = call(coarse_rhs_sums(ncb), [copies], (w2, w1, wi, z2, z1, p, rho, raw_basis), "coarse_rhs_sums", block // 32, [o1], [pltpu.VMEM(*copies), dma(1)], (), (0,))
    early = gather(g)
    m2, m1, _ = margins(h2, h1, o2, o1, g, True)
    p = solve(h2, h1, o2, o1, w, early)
    half = [(layer, F32), ((size, cols // 2), BF), (layer, F32)]
    q2, s2, c2 = call(join_second(2), half, (m2, p, su), "join_second", block)
    q1, s1, c1 = call(join_second(1), half, (m1, p, su), "join_second", block, [s2])
    t2, t1 = swap(2, s2), swap(1, s1)
    q, z, first, sums = call(
        inner_products,
        [(whole, F32), (whole, F32), ((PAD, cols), F32), ((4, cols), F32)],
        (q2, q1, o2, o1, p, z, r, w, sd, su, early),
        "inner_products",
        12 * block,
    )
    (g,) = call(join_sums, [((devices, 4, cols), F32)], (t2, t1, c2, c1, sums), "join_sums")
    (x,) = call(finish, [(whole, F32)], (gather(g), first, z, q), "finish")
    return x[:, None]


def solution(mesh):
    split = P("row", "col", None, None)
    return jax.shard_map(on_device, mesh=mesh, in_specs=(split,) * 6 + (P(),), out_specs=split, check_vma=False)
```

```python
import math

import jax
import jax.numpy as jnp
from jax import lax
from jax.experimental import pallas as pl
from jax.experimental.pallas import tpu as pltpu
from jax.sharding import PartitionSpec as P

BF = jnp.bfloat16
F32 = jnp.float32
ALL = ("row", "col")
PAD = 8
LIMIT = 16 * 1024 * 1024
SCHEDULE_COST = 1200


def mm(a, b):
    return lax.dot_general(a, b, (((1,), (0,)), ((), ())), preferred_element_type=F32)


def mmt(a, b):
    return lax.dot_general(a, b, (((0,), (0,)), ((), ())), preferred_element_type=F32)


def colsum(x):
    return jnp.sum(x, axis=0, keepdims=True)


def is_lower(chain):
    return lax.rem(lax.axis_index("row"), 2) == (0 if chain == 2 else 1)


def goes_on(lower):
    row = lax.axis_index("row")
    return jnp.where(lower, row > 0, row < lax.axis_size("row") - 1)


def kept(x, lower):
    return jnp.where(goes_on(lower), x, jnp.zeros_like(x))


def pick(from2, from1):
    low2 = is_lower(2)
    return jnp.where(low2, from2, from1), jnp.where(low2, from1, from2)


def nbytes(shape, dtype):
    return math.prod(shape) * jnp.dtype(dtype).itemsize


def run_copies(pairs, sems):
    copies = [pltpu.make_async_copy(a, b, sems.at[i]) for i, (a, b) in enumerate(pairs)]
    for c in copies:
        c.start()
    for c in copies:
        c.wait()


def call(body, outs, args, name, flops=0, after=(), scratch=(), hbm=(), far=()):
    shapes = [pltpu.HBM(d, t) if i in far else jax.ShapeDtypeStruct(d, t) for i, (d, t) in enumerate(outs)]
    total = sum(nbytes(a.shape, a.dtype) for a in args)
    room = sum(nbytes(a.shape, a.dtype) for i, a in enumerate(args) if i not in hbm)
    room += sum(nbytes(d, t) for i, (d, t) in enumerate(outs) if i not in far)
    room += sum(nbytes(a.shape, a.dtype) for a in scratch if jnp.issubdtype(a.dtype, jnp.floating))
    args = [pltpu.with_memory_space_constraint(a, pltpu.HBM) if i in hbm else a for i, a in enumerate(args)]
    count, late = len(args), len(after)

    def kernel(*refs):
        body(*refs[:count], *refs[count + late :])

    space = lambda i, there: pl.BlockSpec(memory_space=pltpu.HBM if i in there else pltpu.VMEM)
    return pl.pallas_call(
        kernel,
        out_shape=shapes,
        in_specs=[space(i, hbm) for i in range(count)] + [pl.BlockSpec(memory_space=pl.ANY)] * late,
        out_specs=[space(i, far) for i in range(len(outs))],
        scratch_shapes=list(scratch),
        compiler_params=pltpu.CompilerParams(vmem_limit_bytes=max(LIMIT, room + LIMIT // 2)),
        cost_estimate=pl.CostEstimate(flops=flops, bytes_accessed=total, transcendentals=0),
        name=name,
    )(*args, *after)


def load_edge(chain):
    def body(r, s, *rest):
        whole, sems = rest[:-1], rest[-1]
        edge = (r.at[jnp.where(is_lower(chain), 0, r.shape[0] - 1)], s)
        run_copies([edge] + [(r, to) for to in whole], sems)

    return body


def load_outer(ld, lu, o2, o1, d2, u2, d1, u1, v2, v1, sems):
    lower = is_lower(2)
    at = [jnp.where(lower, 0, m.shape[0] - 1) for m in (ld, lu)]
    to = [m.shape[0] - 1 - i for m, i in zip((ld, lu), at)]
    blocks = [(ld.at[at[0]], d2), (lu.at[at[1]], u2), (ld.at[to[0]], d1), (lu.at[to[1]], u1)]
    run_copies(blocks + [(o2, v2), (o1, v1)], sems)


def margin_solve(chain):
    def body(h, e, diag, upper, s, far, sem):
        lower = is_lower(chain)
        out = pltpu.make_async_copy(h, far, sem)
        out.start()

        @pl.when(lower)
        def _():
            s[...] = (mm(diag[...], h[...]) + mm(upper[...], e[...])).astype(BF)

        @pl.when(jnp.logical_not(lower))
        def _():
            s[...] = (mm(diag[...], h[...]) + mmt(upper[...], e[...])).astype(BF)

        out.wait()

    return body


def solve_layers(*refs):
    far, p, scalars, near, sems = refs[:11], refs[11], refs[12:-12], refs[-12:-1], refs[-1]
    copies = [pltpu.make_async_copy(a, b, sems.at[i]) for i, (a, b) in enumerate(zip(far, near))]
    for c in copies:
        c.start()
    gathered, fpad, fown, basis, h2, h1, o2, o1, e, ld, lu = near
    for c in copies[:4]:
        c.wait()
    g = gathered[...].reshape(-1, gathered.shape[-1])[:, : p.shape[2]]
    v = mm(fpad[...], g).astype(BF)
    u = mmt(fown[...], v).astype(BF)
    size = p.shape[1]
    for c in copies[4:10]:
        c.wait()
    e0, e5 = pick(h2[...], h1[...])
    e0, e5 = kept(e0, True), kept(e5, False)
    e1, e4 = pick(o2[...], o1[...])
    e2, e3 = e[1], e[2]
    for k, x in enumerate((e1, e2, e3, e4)):
        p[k] = mm(ld[k + 1], x) + mmt(basis[:, k * size : (k + 1) * size], u)
    copies[10].wait()
    p[0] = p[0] + mm(lu[1], e2) + mmt(lu[0], e0)
    p[1] = p[1] + mm(lu[2], e3) + mmt(lu[1], e1)
    p[2] = p[2] + mm(lu[3], e4) + mmt(lu[2], e2)
    p[3] = p[3] + mm(lu[4], e5) + mmt(lu[3], e3)
    for out in scalars:
        total = gathered[0].astype(F32)
        for k in range(1, gathered.shape[0]):
            total = total + gathered[k].astype(F32)
        beside = total[:, p.shape[2] :]
        rho, d0 = (
            jnp.concatenate([beside[k : k + 1] + beside[k + 2 : k + 3], beside[k + 1 : k + 2] + beside[k + 3 : k + 4]], axis=1)
            for k in (0, 4)
        )
        out[...] = jnp.concatenate([rho, d0, rho / d0], axis=0)


def join_margin(chain):
    def body(m, p, su, z, s):
        lower = is_lower(chain)
        edge = p[jnp.where(lower, 0, 3)] + kept(m[...], lower).astype(F32)
        z[...] = edge
        s[...] = edge.astype(BF)

        @pl.when(jnp.logical_not(lower))
        def _():
            s[...] = mmt(su[3], edge.astype(BF)).astype(BF)

    return body


def inner_operate(z2, z1, p, r, sd, su, z, w, wb, sums):
    z[0], z[3] = pick(z2[...], z1[...])
    z[1] = p[1]
    z[2] = p[2]
    rho = d0 = jnp.zeros((1, p.shape[2]), F32)
    for k in range(4):
        zk = z[k]
        rho = rho + colsum(r[k].astype(F32) * zk)
        w[k] = mm(sd[k], zk.astype(BF))
        if k < 3:
            w[k] = w[k] + mm(su[k], z[k + 1].astype(BF))
        if k > 0:
            w[k] = w[k] + mmt(su[k - 1], z[k - 1].astype(BF))
        wb[k] = w[k].astype(BF)
        if 0 < k < 3:
            d0 = d0 + colsum(w[k] * zk)
    sums[...] = jnp.concatenate([rho, d0], axis=0)


def join_operate(chain):
    def body(n, w, su, s):
        lower = is_lower(chain)
        term = kept(n[...], lower)

        @pl.when(lower)
        def _():
            s[...] = (w[0] + term.astype(F32)).astype(BF)

        @pl.when(jnp.logical_not(lower))
        def _():
            s[...] = (w[3] + mm(su[3], term)).astype(BF)

    return body


def coarse_rhs(ncb):
    def body(e, basis, g, block, sems):
        out = mm(basis[...], e[...].reshape(-1, e.shape[-1]))
        out = jnp.concatenate([out, jnp.zeros((PAD - ncb, out.shape[1]), F32)], axis=0).astype(BF)
        for k in range(g.shape[0]):
            block[k] = out
        run_copies([(block, g)], sems)

    return body


def prepare(ncb):
    def body(basis, factor, padded_far, fpad_far, fown_far, padded, fpad, fown, sems):
        rows = basis[...].astype(F32)
        padded[...] = jnp.concatenate([rows, jnp.zeros((PAD - ncb, rows.shape[1]), F32)], axis=0).astype(BF)
        nco = factor.shape[0]
        own = lax.axis_index("row") * lax.axis_size("col") + lax.axis_index("col")

        def columns(first, width):
            source = lax.broadcasted_iota(jnp.int32, (nco, width), 0)
            target = lax.broadcasted_iota(jnp.int32, (nco, width), 1)
            at = lax.rem(target, PAD)
            match = (source == (first + target // PAD) * ncb + at) & (at < ncb)
            chosen = jnp.where(match, 1.0, 0.0).astype(BF)
            return mm(factor[...], chosen).astype(BF)

        fown[...] = columns(own, PAD)
        width = 128

        def step(i, carry):
            fpad[:, pl.ds(pl.multiple_of(i * width, width), width)] = columns(i * (width // PAD), width)
            return carry

        lax.fori_loop(0, fpad.shape[1] // width, step, 0)
        run_copies([(padded, padded_far), (fpad, fpad_far), (fown, fown_far)], sems)

    return body


def in_two(x):
    top = x.astype(BF).astype(F32)
    half = x.shape[1] // 2
    return [part[:, at : at + half] for part in (top, x - top) for at in (0, half)]


def coarse_rhs_joined(ncb):
    def body(w2, w1, z2, z1, w, sums, basis, g, block, sems):
        ends, tops = pick(w2[...], w1[...]), pick(z2[...], z1[...])
        size = w.shape[1]
        out = jnp.zeros((ncb, w.shape[2]), F32)
        d0 = sums[1:2]
        for k in range(4):
            wk = w[k].astype(BF) if 0 < k < 3 else ends[k // 3]
            out = out + mm(basis[:, k * size : (k + 1) * size], wk)
        for x, y in zip(ends, tops):
            d0 = d0 + colsum(x.astype(F32) * y)
        out = jnp.concatenate([out, jnp.zeros((PAD - ncb, out.shape[1]), F32)], axis=0)
        beside = jnp.concatenate(in_two(sums[0:1]) + in_two(d0), axis=0)
        out = jnp.concatenate([out, beside], axis=1).astype(BF)
        for k in range(g.shape[0]):
            block[k] = out
        run_copies([(block, g)], sems)

    return body


def join_second(chain):
    def body(m, p, su, q, s, product):
        lower = is_lower(chain)
        half = s.shape[1]
        edge = p[jnp.where(lower, 0, 3)] + kept(m[...], lower).astype(F32)
        q[...] = edge
        product[...] = edge

        @pl.when(lower)
        def _():
            s[...] = edge[:, :half].astype(BF)

        @pl.when(jnp.logical_not(lower))
        def _():
            out = 2.0 * mmt(su[3], edge.astype(BF))
            product[...] = out
            s[...] = out[:, half:].astype(BF)

    return body


def inner_products(q2, q1, o2, o1, p, z, r, w, sd, su, scalars, q, kept_z, sums):
    q[0], q[3] = pick(q2[...], q1[...])
    q[1] = p[1]
    q[2] = p[2]
    ends = pick(o2[...], o1[...])
    kept_z[...] = z[...]
    a0 = scalars[2:3]
    s1 = s2 = s4 = s5 = jnp.zeros((1, q.shape[-1]), F32)
    for k in range(4):
        qk = q[k]
        qb = qk.astype(BF)
        wk = (w[k] if 0 < k < 3 else ends[k // 3]).astype(F32)
        zk = z[k]
        own = mm(sd[k], qb)
        s5 = s5 + colsum(qk * own)
        s4 = s4 + colsum(zk * own)
        s4 = s4 + colsum((wk + wk - mm(sd[k], zk.astype(BF))) * qk)
        if k < 3:
            s5 = s5 + 2.0 * colsum(qk * mm(su[k], q[k + 1].astype(BF)))
        s1 = s1 + colsum(r[k].astype(F32) * qk)
        s2 = s2 + colsum(wk * qk)
    sums[...] = jnp.concatenate([a0 * (a0 * s2 - s1), s4, s5], axis=0)


def join_sums(t2, t1, c2, c1, sums, out):
    low_in, high_in = pick(t2[...], t1[...])
    low, high = pick(c2[...], c1[...])
    half = low_in.shape[1]
    above = colsum(high[:, :half] * kept(high_in, False).astype(F32))
    below = colsum(low[:, half:] * kept(low_in, True).astype(F32))
    right = jnp.concatenate([sums[2:3, :half] + above, sums[2:3, half:] + below], axis=0)
    full = jnp.concatenate([sums[0:2], right], axis=1)
    for k in range(out.shape[0]):
        out[k] = full


def finish(parts, scalars, z, q, x):
    total = parts[0]
    for k in range(1, parts.shape[0]):
        total = total + parts[k]
    cols = z.shape[2]
    rho0, d0, a0 = (scalars[k : k + 1] for k in range(3))
    rho1, s4 = total[0:1, :cols], total[1:2, :cols]
    s5 = jnp.concatenate([total[0:1, cols:], total[1:2, cols:]], axis=1)
    grow = 1.0 + rho1 / rho0
    a1 = rho1 / (grow * grow * d0 - grow * a0 * s4 + a0 * a0 * s5)
    cz = a0 + a1 * grow
    cq = a1 * a0
    for k in range(4):
        x[k] = cz * z[k] - cq * q[k]


def swap(chain, x):
    rows, cols = lax.axis_size("row"), lax.axis_size("col")
    moves = []
    for row in range(rows):
        other = row + 1 if (row % 2 == 0) == (chain == 1) else row - 1
        for col in range(cols):
            inside = 0 <= other < rows
            to = (other, col) if inside else (row, min(col ^ 1, cols - 1))
            moves.append((row * cols + col, to[0] * cols + to[1]))
    return lax.ppermute(x, ALL, moves)


def gather(copies):
    return lax.all_to_all(copies, ALL, 0, 0)


def on_device(rhs, stiff_diag, stiff_upper, local_diag, local_upper, coarse_basis, coarse_factor):
    layers, _, size, cols = rhs.shape
    devices = lax.axis_size("row") * lax.axis_size("col")
    ncb, nco = coarse_basis.shape[2], coarse_factor.shape[0]
    layer, whole = (size, cols), (layers, size, cols)
    copies = ((devices, PAD, cols), BF)
    edge = [(layer, F32), (layer, BF)]
    block = 2 * size * size * cols
    dma = lambda n: pltpu.SemaphoreType.DMA((n,))
    r, sd, su, ld, lu = rhs[:, 0], stiff_diag[:, 0], stiff_upper[:, 0], local_diag[:, 0], local_upper[:, 0]
    raw_basis = coarse_basis[0, 0]

    def margins(h2, h1, o2, o1, g):
        g = pltpu.with_memory_space_constraint(g, pltpu.HBM)
        shapes = [((size, size), BF)] * 4 + [(layer, BF)] * 2
        d2, u2, d1, u1, v2, v1 = call(
            load_outer, shapes, (ld, lu, o2, o1), "load_outer", SCHEDULE_COST * block, [g], [dma(6)], range(4)
        )
        take = lambda chain, args, after: call(
            margin_solve(chain), [(layer, BF)] * 2, args, "margin_solve", 2 * block, after, [pltpu.SemaphoreType.DMA], (), (1,)
        )
        s2, h2 = take(2, (h2, v2, d2, u2), [])
        s1, h1 = take(1, (h1, v1, d1, u1), [s2])
        return swap(2, s2), swap(1, s1), h2, h1, s1

    def solve(h2, h1, o2, o1, e, gathered, scalars):
        args = (gathered, fpad, fown, basis, h2, h1, o2, o1, e, ld, lu)
        held = [pltpu.VMEM(a.shape, a.dtype) for a in args] + [dma(len(args))]
        outs = [(whole, F32)] + [((3, cols), F32)] * scalars
        return call(solve_layers, outs, args, "solve_layers", 12 * block, (), held, range(len(args)))

    (s2,) = call(load_edge(2), [(layer, BF)], (r,), "load_edge", 0, (), [dma(1)], (0,))
    h2 = swap(2, s2)
    s1, near_r = call(load_edge(1), [(layer, BF), (whole, BF)], (r,), "load_edge", 0, [s2], [dma(2)], (0,))
    h1 = swap(1, s1)
    held = [pltpu.VMEM(*copies), dma(1)]
    (g,) = call(coarse_rhs(ncb), [copies], (near_r, raw_basis), "coarse_rhs", block // 32, [s1], held, (), (0,))
    gathered = gather(g)
    m2, m1, h2, h1, last = margins(h2, h1, s2, s1, g)
    shapes = [((PAD, layers * size), BF), ((nco, devices * PAD), BF), ((nco, PAD), BF)]
    held = [pltpu.VMEM(*shape) for shape in shapes] + [dma(3)]
    basis, fpad, fown = call(
        prepare(ncb), shapes, (raw_basis, coarse_factor), "prepare", block // 8, [last], held, (), (0, 1, 2)
    )
    (p,) = solve(h2, h1, s2, s1, r, gathered, 0)
    z2, s2 = call(join_margin(2), edge, (m2, p, su), "join_margin", block)
    z1, s1 = call(join_margin(1), edge, (m1, p, su), "join_margin", block, [s2])
    n2, n1 = swap(2, s2), swap(1, s1)
    outs = [(whole, F32)] * 2 + [(whole, BF), ((2, cols), F32)]
    z, wi, w, sums = call(inner_operate, outs, (z2, z1, p, r, sd, su), "inner_operate", 10 * block)
    (o2,) = call(join_operate(2), edge[1:], (n2, wi, su), "join_operate", block, [n1])
    (o1,) = call(join_operate(1), edge[1:], (n1, wi, su), "join_operate", block, [o2])
    h2, h1 = swap(2, o2), swap(1, o1)
    wider = ((devices, PAD, cols + cols // 2), BF)
    held = [pltpu.VMEM(*wider), dma(1)]
    args = (o2, o1, z2, z1, wi, sums, raw_basis)
    (g,) = call(coarse_rhs_joined(ncb), [wider], args, "coarse_rhs_joined", block // 32, [], held, (), (0,))
    early = gather(g)
    m2, m1, h2, h1, _ = margins(h2, h1, o2, o1, g)
    p, scalars = solve(h2, h1, o2, o1, w, early, 1)
    half = [(layer, F32), ((size, cols // 2), BF), (layer, F32)]
    q2, s2, c2 = call(join_second(2), half, (m2, p, su), "join_second", block)
    q1, s1, c1 = call(join_second(1), half, (m1, p, su), "join_second", block, [s2])
    t2, t1 = swap(2, s2), swap(1, s1)
    q, z, sums = call(
        inner_products,
        [(whole, F32), (whole, F32), ((3, cols), F32)],
        (q2, q1, o2, o1, p, z, r, w, sd, su, scalars),
        "inner_products",
        12 * block,
    )
    (g,) = call(join_sums, [((devices, 2, cols + cols // 2), F32)], (t2, t1, c2, c1, sums), "join_sums")
    (x,) = call(finish, [(whole, F32)], (gather(g), scalars, z, q), "finish")
    return x[:, None]


def solution(mesh):
    split = P("row", "col", None, None)
    return jax.shard_map(on_device, mesh=mesh, in_specs=(split,) * 6 + (P(),), out_specs=split, check_vma=False)
```

```python
import math

import jax
import jax.numpy as jnp
from jax import lax
from jax.experimental import pallas as pl
from jax.experimental.pallas import tpu as pltpu
from jax.sharding import PartitionSpec as P

BF = jnp.bfloat16
F32 = jnp.float32
ALL = ("row", "col")
PAD = 8
LIMIT = 16 * 1024 * 1024
SCHEDULE_COST = 1200


def mm(a, b):
    return lax.dot_general(a, b, (((1,), (0,)), ((), ())), preferred_element_type=F32)


def mmt(a, b):
    return lax.dot_general(a, b, (((0,), (0,)), ((), ())), preferred_element_type=F32)


def colsum(x):
    return jnp.sum(x, axis=0, keepdims=True)


def is_lower(chain):
    return lax.rem(lax.axis_index("row"), 2) == (0 if chain == 2 else 1)


def goes_on(lower):
    row = lax.axis_index("row")
    return jnp.where(lower, row > 0, row < lax.axis_size("row") - 1)


def kept(x, lower):
    return jnp.where(goes_on(lower), x, jnp.zeros_like(x))


def pick(from2, from1):
    low2 = is_lower(2)
    return jnp.where(low2, from2, from1), jnp.where(low2, from1, from2)


def nbytes(shape, dtype):
    return math.prod(shape) * jnp.dtype(dtype).itemsize


def run_copies(pairs, sems):
    copies = [pltpu.make_async_copy(a, b, sems.at[i]) for i, (a, b) in enumerate(pairs)]
    for c in copies:
        c.start()
    for c in copies:
        c.wait()


def call(body, outs, args, name, flops=0, after=(), scratch=(), hbm=(), far=()):
    shapes = [pltpu.HBM(d, t) if i in far else jax.ShapeDtypeStruct(d, t) for i, (d, t) in enumerate(outs)]
    total = sum(nbytes(a.shape, a.dtype) for a in args)
    room = sum(nbytes(a.shape, a.dtype) for i, a in enumerate(args) if i not in hbm)
    room += sum(nbytes(d, t) for i, (d, t) in enumerate(outs) if i not in far)
    room += sum(nbytes(a.shape, a.dtype) for a in scratch if jnp.issubdtype(a.dtype, jnp.floating))
    args = [pltpu.with_memory_space_constraint(a, pltpu.HBM) if i in hbm else a for i, a in enumerate(args)]
    count, late = len(args), len(after)

    def kernel(*refs):
        body(*refs[:count], *refs[count + late :])

    space = lambda i, there: pl.BlockSpec(memory_space=pltpu.HBM if i in there else pltpu.VMEM)
    return pl.pallas_call(
        kernel,
        out_shape=shapes,
        in_specs=[space(i, hbm) for i in range(count)] + [pl.BlockSpec(memory_space=pl.ANY)] * late,
        out_specs=[space(i, far) for i in range(len(outs))],
        scratch_shapes=list(scratch),
        compiler_params=pltpu.CompilerParams(vmem_limit_bytes=max(LIMIT, room + LIMIT // 2)),
        cost_estimate=pl.CostEstimate(flops=flops, bytes_accessed=total, transcendentals=0),
        name=name,
    )(*args, *after)


def load_edge(chain):
    def body(r, s, *rest):
        whole, sems = rest[:-1], rest[-1]
        edge = (r.at[jnp.where(is_lower(chain), 0, r.shape[0] - 1)], s)
        run_copies([edge] + [(r, to) for to in whole], sems)

    return body


def load_outer(ld, lu, o2, o1, d2, u2, d1, u1, v2, v1, sems):
    lower = is_lower(2)
    at = [jnp.where(lower, 0, m.shape[0] - 1) for m in (ld, lu)]
    to = [m.shape[0] - 1 - i for m, i in zip((ld, lu), at)]
    blocks = [(ld.at[at[0]], d2), (lu.at[at[1]], u2), (ld.at[to[0]], d1), (lu.at[to[1]], u1)]
    run_copies(blocks + [(o2, v2), (o1, v1)], sems)


def margin_solve(chain, fetch):
    def body(h, e, diag, upper, s, *rest):
        lower = is_lower(chain)
        out = None
        if fetch:
            run_copies([(h, rest[0])], rest[1])
            h = rest[0]
        elif rest:
            out = pltpu.make_async_copy(h, rest[0], rest[1].at[0])
            out.start()

        @pl.when(lower)
        def _():
            s[...] = (mm(diag[...], h[...]) + mm(upper[...], e[...])).astype(BF)

        @pl.when(jnp.logical_not(lower))
        def _():
            s[...] = (mm(diag[...], h[...]) + mmt(upper[...], e[...])).astype(BF)

        if out is not None:
            out.wait()

    return body


def coarse_values(gathered, factor, compact, ncb):
    devices, _, width = gathered.shape
    cols = compact.shape[1]
    group = math.gcd(devices, 16)
    target = lax.broadcasted_iota(jnp.int32, (group * ncb, group * PAD), 0)
    source = lax.broadcasted_iota(jnp.int32, (group * ncb, group * PAD), 1)
    match = (target // ncb == source // PAD) & (lax.rem(target, ncb) == lax.rem(source, PAD))
    chosen = jnp.where(match, 1.0, 0.0).astype(BF)
    for i in range(devices // group):
        part = gathered[i * group : (i + 1) * group].reshape(group * PAD, width)[:, :cols]
        compact[i * group * ncb : (i + 1) * group * ncb] = mm(chosen, part).astype(BF)
    nco = factor.shape[0]
    own = lax.axis_index("row") * lax.axis_size("col") + lax.axis_index("col")
    row = lax.broadcasted_iota(jnp.int32, (nco, PAD), 0)
    at = lax.broadcasted_iota(jnp.int32, (nco, PAD), 1)
    mine = jnp.where((row == own * ncb + at) & (at < ncb), 1.0, 0.0).astype(BF)
    v = mm(factor[...], compact[...]).astype(BF)
    return mmt(mm(factor[...], mine).astype(BF), v).astype(BF)


def solve_layers(*refs):
    far, p, scalars, near, sems = refs[:11], refs[11], refs[12:-12], refs[-12:-1], refs[-1]
    copies = [pltpu.make_async_copy(a, b, sems.at[i]) for i, (a, b) in enumerate(zip(far, near))]
    for c in copies:
        c.start()
    gathered, fpad, fown, basis, h2, h1, o2, o1, e, ld, lu = near
    for c in copies[:4]:
        c.wait()
    g = gathered[...].reshape(-1, gathered.shape[-1])[:, : p.shape[2]]
    v = mm(fpad[...], g).astype(BF)
    u = mmt(fown[...], v).astype(BF)
    size = p.shape[1]
    for c in copies[4:10]:
        c.wait()
    e0, e5 = pick(h2[...], h1[...])
    e0, e5 = kept(e0, True), kept(e5, False)
    e1, e4 = pick(o2[...], o1[...])
    e2, e3 = e[1], e[2]
    for k, x in enumerate((e1, e2, e3, e4)):
        p[k] = mm(ld[k + 1], x) + mmt(basis[:, k * size : (k + 1) * size], u)
    copies[10].wait()
    p[0] = p[0] + mm(lu[1], e2) + mmt(lu[0], e0)
    p[1] = p[1] + mm(lu[2], e3) + mmt(lu[1], e1)
    p[2] = p[2] + mm(lu[3], e4) + mmt(lu[2], e2)
    p[3] = p[3] + mm(lu[4], e5) + mmt(lu[3], e3)
    for out in scalars:
        total = gathered[0].astype(F32)
        for k in range(1, gathered.shape[0]):
            total = total + gathered[k].astype(F32)
        beside = total[:, p.shape[2] :]
        rho, d0 = (
            jnp.concatenate([beside[k : k + 1] + beside[k + 2 : k + 3], beside[k + 1 : k + 2] + beside[k + 3 : k + 4]], axis=1)
            for k in (0, 4)
        )
        out[...] = jnp.concatenate([rho, d0, rho / d0], axis=0)


def join_margin(chain):
    def body(m, p, su, z, s):
        lower = is_lower(chain)
        edge = p[jnp.where(lower, 0, 3)] + kept(m[...], lower).astype(F32)
        z[...] = edge
        s[...] = edge.astype(BF)

        @pl.when(jnp.logical_not(lower))
        def _():
            s[...] = mmt(su[3], edge.astype(BF)).astype(BF)

    return body


def inner_operate(z2, z1, p, r, sd, su, z, w, wb, sums):
    z[0], z[3] = pick(z2[...], z1[...])
    z[1] = p[1]
    z[2] = p[2]
    rho = d0 = jnp.zeros((1, p.shape[2]), F32)
    for k in range(4):
        zk = z[k]
        rho = rho + colsum(r[k].astype(F32) * zk)
        w[k] = mm(sd[k], zk.astype(BF))
        if k < 3:
            w[k] = w[k] + mm(su[k], z[k + 1].astype(BF))
        if k > 0:
            w[k] = w[k] + mmt(su[k - 1], z[k - 1].astype(BF))
        wb[k] = w[k].astype(BF)
        if 0 < k < 3:
            d0 = d0 + colsum(w[k] * zk)
    sums[...] = jnp.concatenate([rho, d0], axis=0)


def join_operate(chain):
    def body(n, w, su, s):
        lower = is_lower(chain)
        term = kept(n[...], lower)

        @pl.when(lower)
        def _():
            s[...] = (w[0] + term.astype(F32)).astype(BF)

        @pl.when(jnp.logical_not(lower))
        def _():
            s[...] = (w[3] + mm(su[3], term)).astype(BF)

    return body


def coarse_rhs(ncb):
    def body(e, basis, g, block, sems):
        out = mm(basis[...], e[...].reshape(-1, e.shape[-1]))
        out = jnp.concatenate([out, jnp.zeros((PAD - ncb, out.shape[1]), F32)], axis=0).astype(BF)
        for k in range(g.shape[0]):
            block[k] = out
        run_copies([(block, g)], sems)

    return body


def prepare(ncb):
    def body(basis, factor, padded_far, fpad_far, fown_far, padded, fpad, fown, sems):
        rows = basis[...].astype(F32)
        padded[...] = jnp.concatenate([rows, jnp.zeros((PAD - ncb, rows.shape[1]), F32)], axis=0).astype(BF)
        nco = factor.shape[0]
        own = lax.axis_index("row") * lax.axis_size("col") + lax.axis_index("col")

        def columns(first, width):
            source = lax.broadcasted_iota(jnp.int32, (nco, width), 0)
            target = lax.broadcasted_iota(jnp.int32, (nco, width), 1)
            at = lax.rem(target, PAD)
            match = (source == (first + target // PAD) * ncb + at) & (at < ncb)
            chosen = jnp.where(match, 1.0, 0.0).astype(BF)
            return mm(factor[...], chosen).astype(BF)

        fown[...] = columns(own, PAD)
        width = 128

        def step(i, carry):
            fpad[:, pl.ds(pl.multiple_of(i * width, width), width)] = columns(i * (width // PAD), width)
            return carry

        lax.fori_loop(0, fpad.shape[1] // width, step, 0)
        run_copies([(padded, padded_far), (fpad, fpad_far), (fown, fown_far)], sems)

    return body


def in_two(x):
    top = x.astype(BF).astype(F32)
    half = x.shape[1] // 2
    return [part[:, at : at + half] for part in (top, x - top) for at in (0, half)]


def coarse_rhs_joined(ncb):
    def body(w2, w1, z2, z1, w, sums, basis, g, block, sems):
        ends, tops = pick(w2[...], w1[...]), pick(z2[...], z1[...])
        size = w.shape[1]
        out = jnp.zeros((ncb, w.shape[2]), F32)
        d0 = sums[1:2]
        for k in range(4):
            wk = w[k].astype(BF) if 0 < k < 3 else ends[k // 3]
            out = out + mm(basis[:, k * size : (k + 1) * size], wk)
        for x, y in zip(ends, tops):
            d0 = d0 + colsum(x.astype(F32) * y)
        out = jnp.concatenate([out, jnp.zeros((PAD - ncb, out.shape[1]), F32)], axis=0)
        beside = jnp.concatenate(in_two(sums[0:1]) + in_two(d0), axis=0)
        out = jnp.concatenate([out, beside], axis=1).astype(BF)
        for k in range(g.shape[0]):
            block[k] = out
        run_copies([(block, g)], sems)

    return body


def join_second(chain):
    def body(m, p, su, q, s, product):
        lower = is_lower(chain)
        half = s.shape[1]
        edge = p[jnp.where(lower, 0, 3)] + kept(m[...], lower).astype(F32)
        q[...] = edge
        product[...] = edge

        @pl.when(lower)
        def _():
            s[...] = edge[:, :half].astype(BF)

        @pl.when(jnp.logical_not(lower))
        def _():
            out = 2.0 * mmt(su[3], edge.astype(BF))
            product[...] = out
            s[...] = out[:, half:].astype(BF)

    return body


def inner_products(q2, q1, o2, o1, p, z, r, w, sd, su, scalars, q, kept_z, sums):
    q[0], q[3] = pick(q2[...], q1[...])
    q[1] = p[1]
    q[2] = p[2]
    ends = pick(o2[...], o1[...])
    kept_z[...] = z[...]
    a0 = scalars[2:3]
    s1 = s2 = s4 = s5 = jnp.zeros((1, q.shape[-1]), F32)
    for k in range(4):
        qk = q[k]
        qb = qk.astype(BF)
        wk = (w[k] if 0 < k < 3 else ends[k // 3]).astype(F32)
        zk = z[k]
        own = mm(sd[k], qb)
        s5 = s5 + colsum(qk * own)
        s4 = s4 + colsum(zk * own)
        s4 = s4 + colsum((wk + wk - mm(sd[k], zk.astype(BF))) * qk)
        if k < 3:
            s5 = s5 + 2.0 * colsum(qk * mm(su[k], q[k + 1].astype(BF)))
        s1 = s1 + colsum(r[k].astype(F32) * qk)
        s2 = s2 + colsum(wk * qk)
    sums[...] = jnp.concatenate([a0 * (a0 * s2 - s1), s4, s5], axis=0)


def join_sums(t2, t1, c2, c1, sums, out):
    low_in, high_in = pick(t2[...], t1[...])
    low, high = pick(c2[...], c1[...])
    half = low_in.shape[1]
    above = colsum(high[:, :half] * kept(high_in, False).astype(F32))
    below = colsum(low[:, half:] * kept(low_in, True).astype(F32))
    right = jnp.concatenate([sums[2:3, :half] + above, sums[2:3, half:] + below], axis=0)
    full = jnp.concatenate([sums[0:2], right], axis=1)
    for k in range(out.shape[0]):
        out[k] = full


def finish(parts, scalars, z, q, x, held, sems):
    total = parts[0]
    for k in range(1, parts.shape[0]):
        total = total + parts[k]
    cols = z.shape[2]
    rho0, d0, a0 = (scalars[k : k + 1] for k in range(3))
    rho1, s4 = total[0:1, :cols], total[1:2, :cols]
    s5 = jnp.concatenate([total[0:1, cols:], total[1:2, cols:]], axis=1)
    grow = 1.0 + rho1 / rho0
    a1 = rho1 / (grow * grow * d0 - grow * a0 * s4 + a0 * a0 * s5)
    cz = a0 + a1 * grow
    cq = a1 * a0
    for k in range(4):
        held[k] = cz * z[k] - cq * q[k]
        pltpu.make_async_copy(held.at[k], x.at[k], sems.at[k]).start()
    for k in range(4):
        pltpu.make_async_copy(held.at[k], x.at[k], sems.at[k]).wait()


def swap(chain, x):
    rows, cols = lax.axis_size("row"), lax.axis_size("col")
    moves = []
    for row in range(rows):
        other = row + 1 if (row % 2 == 0) == (chain == 1) else row - 1
        for col in range(cols):
            inside = 0 <= other < rows
            to = (other, col) if inside else (row, min(col ^ 1, cols - 1))
            moves.append((row * cols + col, to[0] * cols + to[1]))
    return lax.ppermute(x, ALL, moves)


def gather(copies):
    return lax.all_to_all(copies, ALL, 0, 0)


def on_device(rhs, stiff_diag, stiff_upper, local_diag, local_upper, coarse_basis, coarse_factor):
    layers, _, size, cols = rhs.shape
    devices = lax.axis_size("row") * lax.axis_size("col")
    ncb, nco = coarse_basis.shape[2], coarse_factor.shape[0]
    layer, whole = (size, cols), (layers, size, cols)
    copies = ((devices, PAD, cols), BF)
    edge = [(layer, F32), (layer, BF)]
    block = 2 * size * size * cols
    dma = lambda n: pltpu.SemaphoreType.DMA((n,))
    r, sd, su, ld, lu = rhs[:, 0], stiff_diag[:, 0], stiff_upper[:, 0], local_diag[:, 0], local_upper[:, 0]
    raw_basis = coarse_basis[0, 0]

    def margins(h2, h1, o2, o1, g, mode, order=()):
        g = pltpu.with_memory_space_constraint(g, pltpu.HBM)
        shapes = [((size, size), BF)] * 4 + [(layer, BF)] * 2
        d2, u2, d1, u1, v2, v1 = call(
            load_outer, shapes, (ld, lu, o2, o1), "load_outer", SCHEDULE_COST * block, [g], [dma(6)], range(4)
        )
        outs = [(layer, BF)] * (2 if mode == "keep" else 1)
        held = {"keep": [dma(1)], "fetch": [pltpu.VMEM(layer, BF), dma(1)], "plain": []}[mode]
        hbm, far = (0,) if mode == "fetch" else (), (1,) if mode == "keep" else ()
        take = lambda chain, args, after: call(
            margin_solve(chain, mode == "fetch"), outs, args, "margin_solve", 2 * block, after, held, hbm, far
        )
        s2, *k2 = take(2, (h2, v2, d2, u2), order)
        s1, *k1 = take(1, (h1, v1, d1, u1), [s2])
        return swap(2, s2), swap(1, s1), (k2 or [h2])[0], (k1 or [h1])[0], s1

    def solve(h2, h1, o2, o1, e, gathered, scalars):
        args = (gathered, fpad, fown, basis, h2, h1, o2, o1, e, ld, lu)
        held = [pltpu.VMEM(a.shape, a.dtype) for a in args] + [dma(len(args))]
        outs = [(whole, F32)] + [((3, cols), F32)] * scalars
        return call(solve_layers, outs, args, "solve_layers", 12 * block, (), held, range(len(args)))

    (s2,) = call(load_edge(2), [(layer, BF)], (r,), "load_edge", 0, (), [dma(1)], (0,))
    h2 = swap(2, s2)
    s1, near_r = call(load_edge(1), [(layer, BF), (whole, BF)], (r,), "load_edge", 0, [s2], [dma(2)], (0,))
    h1 = swap(1, s1)
    held = [pltpu.VMEM(*copies), dma(1)]
    (g,) = call(coarse_rhs(ncb), [copies], (near_r, raw_basis), "coarse_rhs", block // 32, [s1], held, (), (0,))
    gathered = gather(g)
    m2, m1, h2, h1, last = margins(h2, h1, s2, s1, g, "keep")
    shapes = [((PAD, layers * size), BF), ((nco, devices * PAD), BF), ((nco, PAD), BF)]
    held = [pltpu.VMEM(*shape) for shape in shapes] + [dma(3)]
    basis, fpad, fown = call(
        prepare(ncb), shapes, (raw_basis, coarse_factor), "prepare", block // 8, [last], held, (), (0, 1, 2)
    )
    (p,) = solve(h2, h1, s2, s1, r, gathered, 0)
    z2, s2 = call(join_margin(2), edge, (m2, p, su), "join_margin", block)
    z1, s1 = call(join_margin(1), edge, (m1, p, su), "join_margin", block, [s2])
    n2, n1 = swap(2, s2), swap(1, s1)
    outs = [(whole, F32)] * 2 + [(whole, BF), ((2, cols), F32)]
    z, wi, w, sums = call(inner_operate, outs, (z2, z1, p, r, sd, su), "inner_operate", 10 * block)
    (o2,) = call(join_operate(2), edge[1:], (n2, wi, su), "join_operate", block, [n1])
    (o1,) = call(join_operate(1), edge[1:], (n1, wi, su), "join_operate", block, [o2])
    h2, h1 = swap(2, o2), swap(1, o1)
    wider = ((devices, PAD, cols + cols // 2), BF)
    held = [pltpu.VMEM(*wider), dma(1)]
    args = (o2, o1, z2, z1, wi, sums, raw_basis)
    (g,) = call(coarse_rhs_joined(ncb), [wider], args, "coarse_rhs_joined", block // 32, [], held, (), (0,))
    early = gather(g)
    m2, m1, h2, h1, _ = margins(h2, h1, o2, o1, g, "fetch")
    p, scalars = solve(h2, h1, o2, o1, w, early, 1)
    half = [(layer, F32), ((size, cols // 2), BF), (layer, F32)]
    q2, s2, c2 = call(join_second(2), half, (m2, p, su), "join_second", block)
    q1, s1, c1 = call(join_second(1), half, (m1, p, su), "join_second", block, [s2])
    t2, t1 = swap(2, s2), swap(1, s1)
    q, z, sums = call(
        inner_products,
        [(whole, F32), (whole, F32), ((3, cols), F32)],
        (q2, q1, o2, o1, p, z, r, w, sd, su, scalars),
        "inner_products",
        12 * block,
    )
    (g,) = call(join_sums, [((devices, 2, cols + cols // 2), F32)], (t2, t1, c2, c1, sums), "join_sums")
    (x,) = call(finish, [(whole, F32)], (gather(g), scalars, z, q), "finish", 0, (), [pltpu.VMEM(whole, F32), dma(4)], (), (0,))
    return x[:, None]


def solution(mesh):
    split = P("row", "col", None, None)
    return jax.shard_map(on_device, mesh=mesh, in_specs=(split,) * 6 + (P(),), out_specs=split, check_vma=False)
```

```python
import math

import jax
import jax.numpy as jnp
from jax import lax
from jax.experimental import pallas as pl
from jax.experimental.pallas import tpu as pltpu
from jax.sharding import PartitionSpec as P

BF = jnp.bfloat16
F32 = jnp.float32
ALL = ("row", "col")
PAD = 8
LIMIT = 16 * 1024 * 1024
SCHEDULE_COST = 1200


def mm(a, b):
    return lax.dot_general(a, b, (((1,), (0,)), ((), ())), preferred_element_type=F32)


def mmt(a, b):
    return lax.dot_general(a, b, (((0,), (0,)), ((), ())), preferred_element_type=F32)


def colsum(x):
    return jnp.sum(x, axis=0, keepdims=True)


def is_lower(chain):
    return lax.rem(lax.axis_index("row"), 2) == (0 if chain == 2 else 1)


def goes_on(lower):
    row = lax.axis_index("row")
    return jnp.where(lower, row > 0, row < lax.axis_size("row") - 1)


def kept(x, lower):
    return jnp.where(goes_on(lower), x, jnp.zeros_like(x))


def pick(from2, from1):
    low2 = is_lower(2)
    return jnp.where(low2, from2, from1), jnp.where(low2, from1, from2)


def nbytes(shape, dtype):
    return math.prod(shape) * jnp.dtype(dtype).itemsize


def run_copies(pairs, sems):
    copies = [pltpu.make_async_copy(a, b, sems.at[i]) for i, (a, b) in enumerate(pairs)]
    for c in copies:
        c.start()
    for c in copies:
        c.wait()


def call(body, outs, args, name, flops=0, after=(), scratch=(), hbm=(), far=()):
    shapes = [pltpu.HBM(d, t) if i in far else jax.ShapeDtypeStruct(d, t) for i, (d, t) in enumerate(outs)]
    total = sum(nbytes(a.shape, a.dtype) for a in args)
    room = sum(nbytes(a.shape, a.dtype) for i, a in enumerate(args) if i not in hbm)
    room += sum(nbytes(d, t) for i, (d, t) in enumerate(outs) if i not in far)
    room += sum(nbytes(a.shape, a.dtype) for a in scratch if jnp.issubdtype(a.dtype, jnp.floating))
    args = [pltpu.with_memory_space_constraint(a, pltpu.HBM) if i in hbm else a for i, a in enumerate(args)]
    count, late = len(args), len(after)

    def kernel(*refs):
        body(*refs[:count], *refs[count + late :])

    space = lambda i, there: pl.BlockSpec(memory_space=pltpu.HBM if i in there else pltpu.VMEM)
    return pl.pallas_call(
        kernel,
        out_shape=shapes,
        in_specs=[space(i, hbm) for i in range(count)] + [pl.BlockSpec(memory_space=pl.ANY)] * late,
        out_specs=[space(i, far) for i in range(len(outs))],
        scratch_shapes=list(scratch),
        compiler_params=pltpu.CompilerParams(vmem_limit_bytes=max(LIMIT, room + LIMIT // 2)),
        cost_estimate=pl.CostEstimate(flops=flops, bytes_accessed=total, transcendentals=0),
        name=name,
    )(*args, *after)


def load_edge(chain):
    def body(r, s, *rest):
        whole, sems = rest[:-1], rest[-1]
        edge = (r.at[jnp.where(is_lower(chain), 0, r.shape[0] - 1)], s)
        run_copies([edge] + [(r, to) for to in whole], sems)

    return body


def load_outer(ld, lu, o2, o1, d2, u2, d1, u1, v2, v1, sems):
    lower = is_lower(2)
    at = [jnp.where(lower, 0, m.shape[0] - 1) for m in (ld, lu)]
    to = [m.shape[0] - 1 - i for m, i in zip((ld, lu), at)]
    blocks = [(ld.at[at[0]], d2), (lu.at[at[1]], u2), (ld.at[to[0]], d1), (lu.at[to[1]], u1)]
    run_copies(blocks + [(o2, v2), (o1, v1)], sems)


def margin_solve(chain, fetch):
    def body(h, e, diag, upper, s, *rest):
        lower = is_lower(chain)
        out = None
        if fetch:
            run_copies([(h, rest[0])], rest[1])
            h = rest[0]
        elif rest:
            out = pltpu.make_async_copy(h, rest[0], rest[1].at[0])
            out.start()

        @pl.when(lower)
        def _():
            s[...] = (mm(diag[...], h[...]) + mm(upper[...], e[...])).astype(BF)

        @pl.when(jnp.logical_not(lower))
        def _():
            s[...] = (mm(diag[...], h[...]) + mmt(upper[...], e[...])).astype(BF)

        if out is not None:
            out.wait()

    return body


def solve_layers(*refs):
    far, p, scalars, near, sems = refs[:11], refs[11], refs[12:-12], refs[-12:-1], refs[-1]
    copies = [pltpu.make_async_copy(a, b, sems.at[i]) for i, (a, b) in enumerate(zip(far, near))]
    for c in copies:
        c.start()
    gathered, fpad, fown, basis, h2, h1, o2, o1, e, ld, lu = near
    for c in copies[:4]:
        c.wait()
    g = gathered[:, : p.shape[2]]
    v = mm(fpad[...], g).astype(BF)
    u = mmt(fown[...], v).astype(BF)
    size = p.shape[1]
    for c in copies[4:10]:
        c.wait()
    e0, e5 = pick(h2[...], h1[...])
    e0, e5 = kept(e0, True), kept(e5, False)
    e1, e4 = pick(o2[...], o1[...])
    e2, e3 = e[1], e[2]
    for k, x in enumerate((e1, e2, e3, e4)):
        p[k] = mm(ld[k + 1], x) + mmt(basis[:, k * size : (k + 1) * size], u)
    copies[10].wait()
    p[0] = p[0] + mm(lu[1], e2) + mmt(lu[0], e0)
    p[1] = p[1] + mm(lu[2], e3) + mmt(lu[1], e1)
    p[2] = p[2] + mm(lu[3], e4) + mmt(lu[2], e2)
    p[3] = p[3] + mm(lu[4], e5) + mmt(lu[3], e3)
    for out in scalars:
        total = jnp.sum(gathered[...].astype(F32).reshape(-1, PAD, gathered.shape[1]), axis=0)
        beside = total[:, p.shape[2] :]
        rho, d0 = (
            jnp.concatenate([beside[k : k + 1] + beside[k + 2 : k + 3], beside[k + 1 : k + 2] + beside[k + 3 : k + 4]], axis=1)
            for k in (0, 4)
        )
        out[...] = jnp.concatenate([rho, d0, rho / d0], axis=0)


def join_margin(chain):
    def body(m, p, su, z, s):
        lower = is_lower(chain)
        edge = p[jnp.where(lower, 0, 3)] + kept(m[...], lower).astype(F32)
        z[...] = edge
        s[...] = edge.astype(BF)

        @pl.when(jnp.logical_not(lower))
        def _():
            s[...] = mmt(su[3], edge.astype(BF)).astype(BF)

    return body


def inner_operate(z2, z1, p, r, sd, su, z, w, wb, sums):
    z[0], z[3] = pick(z2[...], z1[...])
    z[1] = p[1]
    z[2] = p[2]
    rho = d0 = jnp.zeros((1, p.shape[2]), F32)
    for k in range(4):
        zk = z[k]
        rho = rho + colsum(r[k].astype(F32) * zk)
        w[k] = mm(sd[k], zk.astype(BF))
        if k < 3:
            w[k] = w[k] + mm(su[k], z[k + 1].astype(BF))
        if k > 0:
            w[k] = w[k] + mmt(su[k - 1], z[k - 1].astype(BF))
        wb[k] = w[k].astype(BF)
        if 0 < k < 3:
            d0 = d0 + colsum(w[k] * zk)
    sums[...] = jnp.concatenate([rho, d0], axis=0)


def join_operate(chain):
    def body(n, w, su, s):
        lower = is_lower(chain)
        term = kept(n[...], lower)

        @pl.when(lower)
        def _():
            s[...] = (w[0] + term.astype(F32)).astype(BF)

        @pl.when(jnp.logical_not(lower))
        def _():
            s[...] = (w[3] + mm(su[3], term)).astype(BF)

    return body


def fill(block, out):
    twice = jnp.concatenate([out, out], axis=0).astype(BF)
    rows = twice.shape[0]
    for k in range(block.shape[0] // rows):
        block[k * rows : (k + 1) * rows] = twice


def coarse_rhs(ncb):
    def body(e, basis, g, block, sems):
        out = mm(basis[...], e[...].reshape(-1, e.shape[-1]))
        out = jnp.concatenate([out, jnp.zeros((PAD - ncb, out.shape[1]), F32)], axis=0)
        fill(block, out)
        run_copies([(block, g)], sems)

    return body


def prepare(ncb):
    def body(basis, factor, padded_far, fpad_far, fown_far, padded, fpad, fown, sems):
        rows = basis[...].astype(F32)
        padded[...] = jnp.concatenate([rows, jnp.zeros((2 * PAD - ncb, rows.shape[1]), F32)], axis=0).astype(BF)
        nco = factor.shape[0]
        own = lax.axis_index("row") * lax.axis_size("col") + lax.axis_index("col")

        def columns(first, width, limit):
            source = lax.broadcasted_iota(jnp.int32, (nco, width), 0)
            target = lax.broadcasted_iota(jnp.int32, (nco, width), 1)
            at = lax.rem(target, PAD)
            match = (source == (first + target // PAD) * ncb + at) & (at < ncb) & (target < limit)
            chosen = jnp.where(match, 1.0, 0.0).astype(BF)
            return mm(factor[...], chosen).astype(BF)

        fown[...] = columns(own, 2 * PAD, ncb)
        width = 128

        def step(i, carry):
            fpad[:, pl.ds(pl.multiple_of(i * width, width), width)] = columns(i * (width // PAD), width, width)
            return carry

        lax.fori_loop(0, fpad.shape[1] // width, step, 0)
        run_copies([(padded, padded_far), (fpad, fpad_far), (fown, fown_far)], sems)

    return body


def in_two(x):
    top = x.astype(BF).astype(F32)
    half = x.shape[1] // 2
    return [part[:, at : at + half] for part in (top, x - top) for at in (0, half)]


def coarse_rhs_joined(ncb):
    def body(w2, w1, z2, z1, w, sums, basis, g, block, sems):
        ends, tops = pick(w2[...], w1[...]), pick(z2[...], z1[...])
        size = w.shape[1]
        out = jnp.zeros((ncb, w.shape[2]), F32)
        d0 = sums[1:2]
        for k in range(4):
            wk = w[k].astype(BF) if 0 < k < 3 else ends[k // 3]
            out = out + mm(basis[:, k * size : (k + 1) * size], wk)
        for x, y in zip(ends, tops):
            d0 = d0 + colsum(x.astype(F32) * y)
        out = jnp.concatenate([out, jnp.zeros((PAD - ncb, out.shape[1]), F32)], axis=0)
        beside = jnp.concatenate(in_two(sums[0:1]) + in_two(d0), axis=0)
        out = jnp.concatenate([out, beside], axis=1)
        fill(block, out)
        run_copies([(block, g)], sems)

    return body


def join_second(chain):
    def body(m, p, su, q, s, product):
        lower = is_lower(chain)
        half = s.shape[1]
        edge = p[jnp.where(lower, 0, 3)] + kept(m[...], lower).astype(F32)
        q[...] = edge
        product[...] = edge

        @pl.when(lower)
        def _():
            s[...] = edge[:, :half].astype(BF)

        @pl.when(jnp.logical_not(lower))
        def _():
            out = 2.0 * mmt(su[3], edge.astype(BF))
            product[...] = out
            s[...] = out[:, half:].astype(BF)

    return body


def inner_products(q2, q1, o2, o1, p, z, r, w, sd, su, scalars, q, kept_z, sums):
    q[0], q[3] = pick(q2[...], q1[...])
    q[1] = p[1]
    q[2] = p[2]
    ends = pick(o2[...], o1[...])
    kept_z[...] = z[...]
    a0 = scalars[2:3]
    s1 = s2 = s4 = s5 = jnp.zeros((1, q.shape[-1]), F32)
    for k in range(4):
        qk = q[k]
        qb = qk.astype(BF)
        wk = (w[k] if 0 < k < 3 else ends[k // 3]).astype(F32)
        zk = z[k]
        own = mm(sd[k], qb)
        s5 = s5 + colsum(qk * own)
        s4 = s4 + colsum(zk * own)
        s4 = s4 + colsum((wk + wk - mm(sd[k], zk.astype(BF))) * qk)
        if k < 3:
            s5 = s5 + 2.0 * colsum(qk * mm(su[k], q[k + 1].astype(BF)))
        s1 = s1 + colsum(r[k].astype(F32) * qk)
        s2 = s2 + colsum(wk * qk)
    sums[...] = jnp.concatenate([a0 * (a0 * s2 - s1), s4, s5], axis=0)


def join_sums(t2, t1, c2, c1, sums, out):
    low_in, high_in = pick(t2[...], t1[...])
    low, high = pick(c2[...], c1[...])
    half = low_in.shape[1]
    above = colsum(high[:, :half] * kept(high_in, False).astype(F32))
    below = colsum(low[:, half:] * kept(low_in, True).astype(F32))
    right = jnp.concatenate([sums[2:3, :half] + above, sums[2:3, half:] + below], axis=0)
    full = jnp.concatenate([sums[0:2], right], axis=1)
    for k in range(out.shape[0]):
        out[k] = full


def finish(parts, scalars, z, q, x, held, sems):
    total = parts[0]
    for k in range(1, parts.shape[0]):
        total = total + parts[k]
    cols = z.shape[2]
    rho0, d0, a0 = (scalars[k : k + 1] for k in range(3))
    rho1, s4 = total[0:1, :cols], total[1:2, :cols]
    s5 = jnp.concatenate([total[0:1, cols:], total[1:2, cols:]], axis=1)
    grow = 1.0 + rho1 / rho0
    a1 = rho1 / (grow * grow * d0 - grow * a0 * s4 + a0 * a0 * s5)
    cz = a0 + a1 * grow
    cq = a1 * a0
    for k in range(4):
        held[k] = cz * z[k] - cq * q[k]
        pltpu.make_async_copy(held.at[k], x.at[k], sems.at[k]).start()
    for k in range(4):
        pltpu.make_async_copy(held.at[k], x.at[k], sems.at[k]).wait()


def swap(chain, x):
    rows, cols = lax.axis_size("row"), lax.axis_size("col")
    moves = []
    for row in range(rows):
        other = row + 1 if (row % 2 == 0) == (chain == 1) else row - 1
        for col in range(cols):
            inside = 0 <= other < rows
            to = (other, col) if inside else (row, min(col ^ 1, cols - 1))
            moves.append((row * cols + col, to[0] * cols + to[1]))
    return lax.ppermute(x, ALL, moves)


def gather(copies):
    return lax.all_to_all(copies, ALL, 0, 0)


def gather_rows(copies):
    rows, width = copies.shape
    return gather(copies.reshape(rows // PAD, PAD, width)).reshape(rows, width)


def on_device(rhs, stiff_diag, stiff_upper, local_diag, local_upper, coarse_basis, coarse_factor):
    layers, _, size, cols = rhs.shape
    devices = lax.axis_size("row") * lax.axis_size("col")
    ncb, nco = coarse_basis.shape[2], coarse_factor.shape[0]
    layer, whole = (size, cols), (layers, size, cols)
    copies = ((devices * PAD, cols), BF)
    edge = [(layer, F32), (layer, BF)]
    block = 2 * size * size * cols
    dma = lambda n: pltpu.SemaphoreType.DMA((n,))
    r, sd, su, ld, lu = rhs[:, 0], stiff_diag[:, 0], stiff_upper[:, 0], local_diag[:, 0], local_upper[:, 0]
    raw_basis = coarse_basis[0, 0]

    def margins(h2, h1, o2, o1, g, mode, order=()):
        g = pltpu.with_memory_space_constraint(g, pltpu.HBM)
        shapes = [((size, size), BF)] * 4 + [(layer, BF)] * 2
        d2, u2, d1, u1, v2, v1 = call(
            load_outer, shapes, (ld, lu, o2, o1), "load_outer", SCHEDULE_COST * block, [g], [dma(6)], range(4)
        )
        outs = [(layer, BF)] * (2 if mode == "keep" else 1)
        held = {"keep": [dma(1)], "fetch": [pltpu.VMEM(layer, BF), dma(1)], "plain": []}[mode]
        hbm, far = (0,) if mode == "fetch" else (), (1,) if mode == "keep" else ()
        take = lambda chain, args, after: call(
            margin_solve(chain, mode == "fetch"), outs, args, "margin_solve", 2 * block, after, held, hbm, far
        )
        s2, *k2 = take(2, (h2, v2, d2, u2), order)
        s1, *k1 = take(1, (h1, v1, d1, u1), [s2])
        return swap(2, s2), swap(1, s1), (k2 or [h2])[0], (k1 or [h1])[0], s1

    def solve(h2, h1, o2, o1, e, gathered, scalars):
        args = (gathered, fpad, fown, basis, h2, h1, o2, o1, e, ld, lu)
        held = [pltpu.VMEM(a.shape, a.dtype) for a in args] + [dma(len(args))]
        outs = [(whole, F32)] + [((3, cols), F32)] * scalars
        return call(solve_layers, outs, args, "solve_layers", 12 * block, (), held, range(len(args)))

    (s2,) = call(load_edge(2), [(layer, BF)], (r,), "load_edge", 0, (), [dma(1)], (0,))
    h2 = swap(2, s2)
    s1, near_r = call(load_edge(1), [(layer, BF), (whole, BF)], (r,), "load_edge", 0, [s2], [dma(2)], (0,))
    h1 = swap(1, s1)
    held = [pltpu.VMEM(*copies), dma(1)]
    (g,) = call(coarse_rhs(ncb), [copies], (near_r, raw_basis), "coarse_rhs", block // 32, [s1], held, (), (0,))
    gathered = gather_rows(g)
    m2, m1, h2, h1, last = margins(h2, h1, s2, s1, g, "keep")
    shapes = [((2 * PAD, layers * size), BF), ((nco, devices * PAD), BF), ((nco, 2 * PAD), BF)]
    held = [pltpu.VMEM(*shape) for shape in shapes] + [dma(3)]
    basis, fpad, fown = call(
        prepare(ncb), shapes, (raw_basis, coarse_factor), "prepare", block // 8, [last], held, (), (0, 1, 2)
    )
    (p,) = solve(h2, h1, s2, s1, r, gathered, 0)
    z2, s2 = call(join_margin(2), edge, (m2, p, su), "join_margin", block)
    z1, s1 = call(join_margin(1), edge, (m1, p, su), "join_margin", block, [s2])
    n2, n1 = swap(2, s2), swap(1, s1)
    outs = [(whole, F32)] * 2 + [(whole, BF), ((2, cols), F32)]
    z, wi, w, sums = call(inner_operate, outs, (z2, z1, p, r, sd, su), "inner_operate", 10 * block)
    (o2,) = call(join_operate(2), edge[1:], (n2, wi, su), "join_operate", block, [n1])
    (o1,) = call(join_operate(1), edge[1:], (n1, wi, su), "join_operate", block, [o2])
    h2, h1 = swap(2, o2), swap(1, o1)
    wider = ((devices * PAD, cols + cols // 2), BF)
    held = [pltpu.VMEM(*wider), dma(1)]
    args = (o2, o1, z2, z1, wi, sums, raw_basis)
    (g,) = call(coarse_rhs_joined(ncb), [wider], args, "coarse_rhs_joined", block // 32, [], held, (), (0,))
    early = gather_rows(g)
    m2, m1, h2, h1, _ = margins(h2, h1, o2, o1, g, "fetch")
    p, scalars = solve(h2, h1, o2, o1, w, early, 1)
    half = [(layer, F32), ((size, cols // 2), BF), (layer, F32)]
    q2, s2, c2 = call(join_second(2), half, (m2, p, su), "join_second", block)
    q1, s1, c1 = call(join_second(1), half, (m1, p, su), "join_second", block, [s2])
    t2, t1 = swap(2, s2), swap(1, s1)
    q, z, sums = call(
        inner_products,
        [(whole, F32), (whole, F32), ((3, cols), F32)],
        (q2, q1, o2, o1, p, z, r, w, sd, su, scalars),
        "inner_products",
        12 * block,
    )
    (g,) = call(join_sums, [((devices, 2, cols + cols // 2), F32)], (t2, t1, c2, c1, sums), "join_sums")
    (x,) = call(finish, [(whole, F32)], (gather(g), scalars, z, q), "finish", 0, (), [pltpu.VMEM(whole, F32), dma(4)], (), (0,))
    return x[:, None]


def solution(mesh):
    split = P("row", "col", None, None)
    return jax.shard_map(on_device, mesh=mesh, in_specs=(split,) * 6 + (P(),), out_specs=split, check_vma=False)
```

```python
import math

import jax
import jax.numpy as jnp
from jax import lax
from jax.experimental import pallas as pl
from jax.experimental.pallas import tpu as pltpu
from jax.sharding import PartitionSpec as P

BF = jnp.bfloat16
F32 = jnp.float32
ALL = ("row", "col")
PAD = 8
LIMIT = 16 * 1024 * 1024
SCHEDULE_COST = 1200


def mm(a, b):
    return lax.dot_general(a, b, (((1,), (0,)), ((), ())), preferred_element_type=F32)


def mmt(a, b):
    return lax.dot_general(a, b, (((0,), (0,)), ((), ())), preferred_element_type=F32)


def colsum(x):
    return jnp.sum(x, axis=0, keepdims=True)


def is_lower(chain):
    return lax.rem(lax.axis_index("row"), 2) == (0 if chain == 2 else 1)


def goes_on(lower):
    row = lax.axis_index("row")
    return jnp.where(lower, row > 0, row < lax.axis_size("row") - 1)


def kept(x, lower):
    return jnp.where(goes_on(lower), x, jnp.zeros_like(x))


def pick(from2, from1):
    low2 = is_lower(2)
    return jnp.where(low2, from2, from1), jnp.where(low2, from1, from2)


def nbytes(shape, dtype):
    return math.prod(shape) * jnp.dtype(dtype).itemsize


def run_copies(pairs, sems):
    copies = [pltpu.make_async_copy(a, b, sems.at[i]) for i, (a, b) in enumerate(pairs)]
    for c in copies:
        c.start()
    for c in copies:
        c.wait()


def call(body, outs, args, name, flops=0, after=(), scratch=(), hbm=(), far=()):
    shapes = [pltpu.HBM(d, t) if i in far else jax.ShapeDtypeStruct(d, t) for i, (d, t) in enumerate(outs)]
    total = sum(nbytes(a.shape, a.dtype) for a in args)
    room = sum(nbytes(a.shape, a.dtype) for i, a in enumerate(args) if i not in hbm)
    room += sum(nbytes(d, t) for i, (d, t) in enumerate(outs) if i not in far)
    room += sum(nbytes(a.shape, a.dtype) for a in scratch if jnp.issubdtype(a.dtype, jnp.floating))
    args = [pltpu.with_memory_space_constraint(a, pltpu.HBM) if i in hbm else a for i, a in enumerate(args)]
    count, late = len(args), len(after)

    def kernel(*refs):
        body(*refs[:count], *refs[count + late :])

    space = lambda i, there: pl.BlockSpec(memory_space=pltpu.HBM if i in there else pltpu.VMEM)
    return pl.pallas_call(
        kernel,
        out_shape=shapes,
        in_specs=[space(i, hbm) for i in range(count)] + [pl.BlockSpec(memory_space=pl.ANY)] * late,
        out_specs=[space(i, far) for i in range(len(outs))],
        scratch_shapes=list(scratch),
        compiler_params=pltpu.CompilerParams(vmem_limit_bytes=max(LIMIT, room + LIMIT // 2)),
        cost_estimate=pl.CostEstimate(flops=flops, bytes_accessed=total, transcendentals=0),
        name=name,
    )(*args, *after)


def load_edge(chain):
    def body(r, s, *rest):
        whole, sems = rest[:-1], rest[-1]
        edge = (r.at[jnp.where(is_lower(chain), 0, r.shape[0] - 1)], s)
        run_copies([edge] + [(r, to) for to in whole], sems)

    return body


def load_outer(ld, lu, o2, o1, d2, u2, d1, u1, v2, v1, sems):
    lower = is_lower(2)
    at = [jnp.where(lower, 0, m.shape[0] - 1) for m in (ld, lu)]
    to = [m.shape[0] - 1 - i for m, i in zip((ld, lu), at)]
    blocks = [(ld.at[at[0]], d2), (lu.at[at[1]], u2), (ld.at[to[0]], d1), (lu.at[to[1]], u1)]
    run_copies(blocks + [(o2, v2), (o1, v1)], sems)


def margin_solve(chain, fetch):
    def body(h, e, diag, upper, s, *rest):
        lower = is_lower(chain)
        out = None
        if fetch:
            run_copies([(h, rest[0])], rest[1])
            h = rest[0]
        elif rest:
            out = pltpu.make_async_copy(h, rest[0], rest[1].at[0])
            out.start()

        @pl.when(lower)
        def _():
            s[...] = (mm(diag[...], h[...]) + mm(upper[...], e[...])).astype(BF)

        @pl.when(jnp.logical_not(lower))
        def _():
            s[...] = (mm(diag[...], h[...]) + mmt(upper[...], e[...])).astype(BF)

        if out is not None:
            out.wait()

    return body


def solve_layers(*refs):
    far, p, scalars, near, sems = refs[:11], refs[11], refs[12:-12], refs[-12:-1], refs[-1]
    far = list(far)
    skip = 0 if scalars else 1
    if scalars:
        far[8] = far[8].at[pl.ds(1, 2)]
        far[9] = far[9].at[pl.ds(1, 4)]
    copies = [pltpu.make_async_copy(a, b, sems.at[i]) for i, (a, b) in enumerate(zip(far, near))]
    for c in copies:
        c.start()
    gathered, fpad, fown, basis, h2, h1, o2, o1, e, ld, lu = near
    for c in copies[:4]:
        c.wait()
    g = gathered[:, : p.shape[2]]
    v = mm(fpad[...], g).astype(BF)
    u = mmt(fown[...], v).astype(BF)
    size = p.shape[1]
    for c in copies[4:10]:
        c.wait()
    e0, e5 = pick(h2[...], h1[...])
    e0, e5 = kept(e0, True), kept(e5, False)
    e1, e4 = pick(o2[...], o1[...])
    e2, e3 = e[skip], e[skip + 1]
    for k, x in enumerate((e1, e2, e3, e4)):
        p[k] = mm(ld[k + skip], x) + mmt(basis[:, k * size : (k + 1) * size], u)
    copies[10].wait()
    p[0] = p[0] + mm(lu[1], e2) + mmt(lu[0], e0)
    p[1] = p[1] + mm(lu[2], e3) + mmt(lu[1], e1)
    p[2] = p[2] + mm(lu[3], e4) + mmt(lu[2], e2)
    p[3] = p[3] + mm(lu[4], e5) + mmt(lu[3], e3)
    for out in scalars:
        total = jnp.sum(gathered[...].astype(F32).reshape(-1, PAD, gathered.shape[1]), axis=0)
        beside = total[:, p.shape[2] :]
        rho, d0 = (
            jnp.concatenate([beside[k : k + 1] + beside[k + 2 : k + 3], beside[k + 1 : k + 2] + beside[k + 3 : k + 4]], axis=1)
            for k in (0, 4)
        )
        out[...] = jnp.concatenate([rho, d0, rho / d0], axis=0)


def join_margin(chain):
    def body(m, p, su, z, s):
        lower = is_lower(chain)
        edge = p[jnp.where(lower, 0, 3)] + kept(m[...], lower).astype(F32)
        z[...] = edge
        s[...] = edge.astype(BF)

        @pl.when(jnp.logical_not(lower))
        def _():
            s[...] = mmt(su[3], edge.astype(BF)).astype(BF)

    return body


def inner_operate(z2, z1, p, r, sd, su, z, w, wb, sums):
    z[0], z[3] = pick(z2[...], z1[...])
    z[1] = p[1]
    z[2] = p[2]
    rho = d0 = jnp.zeros((1, p.shape[2]), F32)
    for k in range(4):
        zk = z[k]
        rho = rho + colsum(r[k].astype(F32) * zk)
        w[k] = mm(sd[k], zk.astype(BF))
        if k < 3:
            w[k] = w[k] + mm(su[k], z[k + 1].astype(BF))
        if k > 0:
            w[k] = w[k] + mmt(su[k - 1], z[k - 1].astype(BF))
        wb[k] = w[k].astype(BF)
        if 0 < k < 3:
            d0 = d0 + colsum(w[k] * zk)
    sums[...] = jnp.concatenate([rho, d0], axis=0)


def join_operate(chain):
    def body(n, w, su, s):
        lower = is_lower(chain)
        term = kept(n[...], lower)

        @pl.when(lower)
        def _():
            s[...] = (w[0] + term.astype(F32)).astype(BF)

        @pl.when(jnp.logical_not(lower))
        def _():
            s[...] = (w[3] + mm(su[3], term)).astype(BF)

    return body


def fill(block, out):
    twice = jnp.concatenate([out, out], axis=0).astype(BF)
    rows = twice.shape[0]
    for k in range(block.shape[0] // rows):
        block[k * rows : (k + 1) * rows] = twice


def coarse_rhs(ncb):
    def body(e, basis, g, block, sems):
        out = mm(basis[...], e[...].reshape(-1, e.shape[-1]))
        out = jnp.concatenate([out, jnp.zeros((PAD - ncb, out.shape[1]), F32)], axis=0)
        fill(block, out)
        run_copies([(block, g)], sems)

    return body


def prepare(ncb):
    def body(basis, factor, padded_far, fpad_far, fown_far, padded, fpad, fown, sems):
        rows = basis[...].astype(F32)
        padded[...] = jnp.concatenate([rows, jnp.zeros((2 * PAD - ncb, rows.shape[1]), F32)], axis=0).astype(BF)
        nco = factor.shape[0]
        own = lax.axis_index("row") * lax.axis_size("col") + lax.axis_index("col")

        def columns(first, width, limit):
            source = lax.broadcasted_iota(jnp.int32, (nco, width), 0)
            target = lax.broadcasted_iota(jnp.int32, (nco, width), 1)
            at = lax.rem(target, PAD)
            match = (source == (first + target // PAD) * ncb + at) & (at < ncb) & (target < limit)
            chosen = jnp.where(match, 1.0, 0.0).astype(BF)
            return mm(factor[...], chosen).astype(BF)

        fown[...] = columns(own, 2 * PAD, ncb)
        width = 128

        def step(i, carry):
            fpad[:, pl.ds(pl.multiple_of(i * width, width), width)] = columns(i * (width // PAD), width, width)
            return carry

        lax.fori_loop(0, fpad.shape[1] // width, step, 0)
        run_copies([(padded, padded_far), (fpad, fpad_far), (fown, fown_far)], sems)

    return body


def in_two(x):
    top = x.astype(BF).astype(F32)
    half = x.shape[1] // 2
    return [part[:, at : at + half] for part in (top, x - top) for at in (0, half)]


def coarse_rhs_joined(ncb):
    def body(w2, w1, z2, z1, w, sums, basis, g, block, sems):
        ends, tops = pick(w2[...], w1[...]), pick(z2[...], z1[...])
        size = w.shape[1]
        out = jnp.zeros((ncb, w.shape[2]), F32)
        d0 = sums[1:2]
        for k in range(4):
            wk = w[k].astype(BF) if 0 < k < 3 else ends[k // 3]
            out = out + mm(basis[:, k * size : (k + 1) * size], wk)
        for x, y in zip(ends, tops):
            d0 = d0 + colsum(x.astype(F32) * y)
        out = jnp.concatenate([out, jnp.zeros((PAD - ncb, out.shape[1]), F32)], axis=0)
        beside = jnp.concatenate(in_two(sums[0:1]) + in_two(d0), axis=0)
        out = jnp.concatenate([out, beside], axis=1)
        fill(block, out)
        run_copies([(block, g)], sems)

    return body


def join_second(chain):
    def body(m, p, su, q, s, product):
        lower = is_lower(chain)
        half = s.shape[1]
        edge = p[jnp.where(lower, 0, 3)] + kept(m[...], lower).astype(F32)
        q[...] = edge
        product[...] = edge

        @pl.when(lower)
        def _():
            s[...] = edge[:, :half].astype(BF)

        @pl.when(jnp.logical_not(lower))
        def _():
            out = 2.0 * mmt(su[3], edge.astype(BF))
            product[...] = out
            s[...] = out[:, half:].astype(BF)

    return body


def inner_products(q2, q1, o2, o1, p, z, r, w, sd, su, scalars, q, kept_z, sums):
    q[0], q[3] = pick(q2[...], q1[...])
    q[1] = p[1]
    q[2] = p[2]
    ends = pick(o2[...], o1[...])
    kept_z[...] = z[...]
    a0 = scalars[2:3]
    s1 = s2 = s4 = s5 = jnp.zeros((1, q.shape[-1]), F32)
    for k in range(4):
        qk = q[k]
        qb = qk.astype(BF)
        wk = (w[k] if 0 < k < 3 else ends[k // 3]).astype(F32)
        zk = z[k]
        own = mm(sd[k], qb)
        s5 = s5 + colsum(qk * own)
        s4 = s4 + colsum(zk * own)
        s4 = s4 + colsum((wk + wk - mm(sd[k], zk.astype(BF))) * qk)
        if k < 3:
            s5 = s5 + 2.0 * colsum(qk * mm(su[k], q[k + 1].astype(BF)))
        s1 = s1 + colsum(r[k].astype(F32) * qk)
        s2 = s2 + colsum(wk * qk)
    sums[...] = jnp.concatenate([a0 * (a0 * s2 - s1), s4, s5], axis=0)


def join_sums(t2, t1, c2, c1, sums, out):
    low_in, high_in = pick(t2[...], t1[...])
    low, high = pick(c2[...], c1[...])
    half = low_in.shape[1]
    above = colsum(high[:, :half] * kept(high_in, False).astype(F32))
    below = colsum(low[:, half:] * kept(low_in, True).astype(F32))
    right = jnp.concatenate([sums[2:3, :half] + above, sums[2:3, half:] + below], axis=0)
    full = jnp.concatenate([sums[0:2], right], axis=1)
    for k in range(out.shape[0]):
        out[k] = full


def finish(parts, scalars, z, q, x, held, sems):
    total = parts[0]
    for k in range(1, parts.shape[0]):
        total = total + parts[k]
    cols = z.shape[2]
    rho0, d0, a0 = (scalars[k : k + 1] for k in range(3))
    rho1, s4 = total[0:1, :cols], total[1:2, :cols]
    s5 = jnp.concatenate([total[0:1, cols:], total[1:2, cols:]], axis=1)
    grow = 1.0 + rho1 / rho0
    a1 = rho1 / (grow * grow * d0 - grow * a0 * s4 + a0 * a0 * s5)
    cz = a0 + a1 * grow
    cq = a1 * a0
    for k in range(4):
        held[k] = cz * z[k] - cq * q[k]
        pltpu.make_async_copy(held.at[k], x.at[k], sems.at[k]).start()
    for k in range(4):
        pltpu.make_async_copy(held.at[k], x.at[k], sems.at[k]).wait()


def swap(chain, x):
    rows, cols = lax.axis_size("row"), lax.axis_size("col")
    moves = []
    for row in range(rows):
        other = row + 1 if (row % 2 == 0) == (chain == 1) else row - 1
        for col in range(cols):
            inside = 0 <= other < rows
            to = (other, col) if inside else (row, min(col ^ 1, cols - 1))
            moves.append((row * cols + col, to[0] * cols + to[1]))
    return lax.ppermute(x, ALL, moves)


def gather(copies):
    return lax.all_to_all(copies, ALL, 0, 0)


def gather_rows(copies):
    rows, width = copies.shape
    return gather(copies.reshape(rows // PAD, PAD, width)).reshape(rows, width)


def on_device(rhs, stiff_diag, stiff_upper, local_diag, local_upper, coarse_basis, coarse_factor):
    layers, _, size, cols = rhs.shape
    devices = lax.axis_size("row") * lax.axis_size("col")
    ncb, nco = coarse_basis.shape[2], coarse_factor.shape[0]
    layer, whole = (size, cols), (layers, size, cols)
    copies = ((devices * PAD, cols), BF)
    edge = [(layer, F32), (layer, BF)]
    block = 2 * size * size * cols
    dma = lambda n: pltpu.SemaphoreType.DMA((n,))
    r, sd, su, ld, lu = rhs[:, 0], stiff_diag[:, 0], stiff_upper[:, 0], local_diag[:, 0], local_upper[:, 0]
    raw_basis = coarse_basis[0, 0]

    def margins(h2, h1, o2, o1, g, mode, order=()):
        g = pltpu.with_memory_space_constraint(g, pltpu.HBM)
        shapes = [((size, size), BF)] * 4 + [(layer, BF)] * 2
        d2, u2, d1, u1, v2, v1 = call(
            load_outer, shapes, (ld, lu, o2, o1), "load_outer", SCHEDULE_COST * block, [g], [dma(6)], range(4)
        )
        outs = [(layer, BF)] * (2 if mode == "keep" else 1)
        held = {"keep": [dma(1)], "fetch": [pltpu.VMEM(layer, BF), dma(1)], "plain": []}[mode]
        hbm, far = (0,) if mode == "fetch" else (), (1,) if mode == "keep" else ()
        take = lambda chain, args, after: call(
            margin_solve(chain, mode == "fetch"), outs, args, "margin_solve", 2 * block, after, held, hbm, far
        )
        s2, *k2 = take(2, (h2, v2, d2, u2), order)
        s1, *k1 = take(1, (h1, v1, d1, u1), [s2])
        return swap(2, s2), swap(1, s1), (k2 or [h2])[0], (k1 or [h1])[0], s1

    def solve(h2, h1, o2, o1, e, gathered, scalars):
        args = (gathered, fpad, fown, basis, h2, h1, o2, o1, e, ld, lu)
        shapes = [a.shape for a in args]
        if scalars:
            shapes = shapes[:8] + [(2,) + layer, (4, size, size), lu.shape]
        held = [pltpu.VMEM(shape, BF) for shape in shapes] + [dma(len(args))]
        outs = [(whole, F32)] + [((3, cols), F32)] * scalars
        return call(solve_layers, outs, args, "solve_layers", 12 * block, (), held, range(len(args)))

    (s2,) = call(load_edge(2), [(layer, BF)], (r,), "load_edge", 0, (), [dma(1)], (0,))
    h2 = swap(2, s2)
    s1, near_r = call(load_edge(1), [(layer, BF), (whole, BF)], (r,), "load_edge", 0, [s2], [dma(2)], (0,))
    h1 = swap(1, s1)
    held = [pltpu.VMEM(*copies), dma(1)]
    (g,) = call(coarse_rhs(ncb), [copies], (near_r, raw_basis), "coarse_rhs", block // 32, [s1], held, (), (0,))
    gathered = gather_rows(g)
    m2, m1, h2, h1, last = margins(h2, h1, s2, s1, g, "keep")
    shapes = [((2 * PAD, layers * size), BF), ((nco, devices * PAD), BF), ((nco, 2 * PAD), BF)]
    held = [pltpu.VMEM(*shape) for shape in shapes] + [dma(3)]
    basis, fpad, fown = call(
        prepare(ncb), shapes, (raw_basis, coarse_factor), "prepare", block // 8, [last], held, (), (0, 1, 2)
    )
    (p,) = solve(h2, h1, s2, s1, r, gathered, 0)
    z2, s2 = call(join_margin(2), edge, (m2, p, su), "join_margin", block)
    z1, s1 = call(join_margin(1), edge, (m1, p, su), "join_margin", block, [s2])
    n2, n1 = swap(2, s2), swap(1, s1)
    outs = [(whole, F32)] * 2 + [(whole, BF), ((2, cols), F32)]
    z, wi, w, sums = call(inner_operate, outs, (z2, z1, p, r, sd, su), "inner_operate", 10 * block)
    (o2,) = call(join_operate(2), edge[1:], (n2, wi, su), "join_operate", block, [n1])
    (o1,) = call(join_operate(1), edge[1:], (n1, wi, su), "join_operate", block, [o2])
    h2, h1 = swap(2, o2), swap(1, o1)
    wider = ((devices * PAD, cols + cols // 2), BF)
    held = [pltpu.VMEM(*wider), dma(1)]
    args = (o2, o1, z2, z1, wi, sums, raw_basis)
    (g,) = call(coarse_rhs_joined(ncb), [wider], args, "coarse_rhs_joined", block // 32, [], held, (), (0,))
    early = gather_rows(g)
    m2, m1, h2, h1, _ = margins(h2, h1, o2, o1, g, "fetch")
    p, scalars = solve(h2, h1, o2, o1, w, early, 1)
    half = [(layer, F32), ((size, cols // 2), BF), (layer, F32)]
    q2, s2, c2 = call(join_second(2), half, (m2, p, su), "join_second", block)
    q1, s1, c1 = call(join_second(1), half, (m1, p, su), "join_second", block, [s2])
    t2, t1 = swap(2, s2), swap(1, s1)
    q, z, sums = call(
        inner_products,
        [(whole, F32), (whole, F32), ((3, cols), F32)],
        (q2, q1, o2, o1, p, z, r, w, sd, su, scalars),
        "inner_products",
        12 * block,
    )
    (g,) = call(join_sums, [((devices, 2, cols + cols // 2), F32)], (t2, t1, c2, c1, sums), "join_sums")
    (x,) = call(finish, [(whole, F32)], (gather(g), scalars, z, q), "finish", 0, (), [pltpu.VMEM(whole, F32), dma(4)], (), (0,))
    return x[:, None]


def solution(mesh):
    split = P("row", "col", None, None)
    return jax.shard_map(on_device, mesh=mesh, in_specs=(split,) * 6 + (P(),), out_specs=split, check_vma=False)
```
